512 devices in a mesh: dp: 16 (over x, y_lo), ctx: 32 (over y_hi, z, core).
Axes of the slice: x: 4, y: 8 (y_hi: 2, y_lo: 4; y = y_hi * 4 + y_lo), z: 8, core: 2. Of those that a mesh axis runs over, the one named last changes fastest.
Arguments:
- query: bfloat16 [16, 4096, 4096], P('dp', 'ctx'), may hold values from -5 to 5
- keys: bfloat16 [16, 4096, 512], P('dp', 'ctx'), may hold values from -5 to 5
- values: bfloat16 [16, 4096, 512], P('dp', 'ctx'), may hold values from -6 to 6
- out_grad: bfloat16 [16, 4096, 4096], P('dp', 'ctx'), may hold values from -16 to 16
- query_lowrank_state: bfloat16 [16, 4096, 8], P('dp', 'ctx'), may hold values from -0.0625 to 0.0625
- value_lowrank_state: bfloat16 [16, 4096, 8], P('dp', 'ctx'), may hold values from -0.0625 to 0.0625
- shift_flags: int32 [4], replicated, may hold values from 0 to 1, as said below
Outputs:
- query_gradient: bfloat16 [16, 4096, 4096], P('dp', 'ctx')
- key_gradient: bfloat16 [16, 4096, 512], P('dp', 'ctx')
- value_gradient: bfloat16 [16, 4096, 512], P('dp', 'ctx')
- query_adapter_gradient: float32 [8, 4096], replicated
- value_adapter_gradient: float32 [8, 512], replicated
The draws below stay inside these ranges and needn't reach their ends.
Inputs may be any that keep to these rules, and one draw needn't show every extreme that they name: `shift_flags`: exactly half of the 4 entries are 1, the others 0.
All inputs are finite; a program needn't handle non-finite values.
Results may differ from the reference program's by a relative error of at most 0.012.
Values may be sent and summed in bfloat16 or wider, within the bound.
No kernel may reach another device: no remote copies, remote signals or barrier semaphores. Data moves between devices by JAX's collectives and lax.ppermute only.
A program may use at most 64 MiB of HBM per device.

```python
import math
import jax
import jax.numpy as jnp
from jax import lax

QUERY_HEADS_HALF = 32
KEY_VALUE_HEADS = 4
HEAD_WIDTH = 128
ADAPTER_RANK = 8
TOK_DEV = 128
GROUP_DEV = 8
BATCH = 16
SEQ = 4096
DEVICES = 512


def draw_query(key, part):
    key = jax.random.fold_in(key, 3)
    array_shape = (BATCH, SEQ, KEY_VALUE_HEADS, QUERY_HEADS_HALF // KEY_VALUE_HEADS, HEAD_WIDTH)
    drawn_rows = jax.random.truncated_normal(key, -5.0, 5.0, array_shape, jnp.float32)
    return drawn_rows.reshape(BATCH, SEQ, QUERY_HEADS_HALF * HEAD_WIDTH).astype(jnp.bfloat16)


def draw_keys(key, part):
    key = jax.random.fold_in(key, 5)
    array_shape = (BATCH, SEQ, KEY_VALUE_HEADS, 1, HEAD_WIDTH)
    drawn_rows = jax.random.truncated_normal(key, -5.0, 5.0, array_shape, jnp.float32)
    return drawn_rows.reshape(BATCH, SEQ, KEY_VALUE_HEADS * HEAD_WIDTH).astype(jnp.bfloat16)


def draw_shift_flags(key, part):
    key = jax.random.fold_in(key, 7)
    shuffled = jax.random.permutation(key, KEY_VALUE_HEADS)
    return (shuffled < KEY_VALUE_HEADS // 2).astype(jnp.int32)


def block_levels(key, shape, pieces, low, top_value):
    def one(dim, shards_of):
        heights = jax.random.uniform(jax.random.fold_in(jax.random.fold_in(key, 6), dim), (shards_of,), jnp.float32, low / len(pieces), top_value / len(pieces))
        return jnp.repeat(jnp.exp(heights), shape[dim] // shards_of).reshape((-1,) + (1,) * (len(shape) - dim - 1))

    gain = one(*pieces[0])
    for cut in pieces[1:]:
        gain = gain * one(*cut)
    return gain


def centred(key, dims, scale, limit, shards=(), held_as=jnp.bfloat16):
    result = scale * jax.random.normal(key, dims, jnp.float32)
    if shards:
        result = result * block_levels(key, dims, shards, -0.22, 0.18)
    return jnp.clip(result, -limit, limit).astype(held_as)


def setup_inputs(seed: int = 0) -> dict:
    key_list = jax.random.split(jax.random.key(seed), 8)
    return {
        "query": draw_query(jax.random.fold_in(key_list[7], 71), 0),
        "keys": draw_keys(jax.random.fold_in(key_list[7], 71), 0),
        "values": centred(key_list[2], (BATCH, SEQ, KEY_VALUE_HEADS * HEAD_WIDTH), 1.0, 6.0, ((0, 16), (1, 32))),
        "out_grad": centred(key_list[3], (BATCH, SEQ, QUERY_HEADS_HALF * HEAD_WIDTH), 4.0, 16.0, ((0, 16), (1, 32))),
        "query_lowrank_state": centred(key_list[4], (BATCH, SEQ, ADAPTER_RANK), (3.0 / (TOK_DEV * DEVICES) ** 0.5), 0.0625, ((0, 16), (1, 32))),
        "value_lowrank_state": centred(key_list[5], (BATCH, SEQ, ADAPTER_RANK), (3.0 / (TOK_DEV * DEVICES) ** 0.5), 0.0625, ((0, 16), (1, 32))),
        "shift_flags": draw_shift_flags(jax.random.fold_in(key_list[7], 71), 0),
    }


ADAPTER_SCALE = 2.0

def rope_back(gradient, positions):
    half_dim = gradient.shape[-1] // 2
    inv_freq = 10000.0 ** (-(jnp.arange(half_dim, dtype=jnp.float32) * 2.0) / gradient.shape[-1])
    angles = positions.astype(jnp.float32)[:, None] * inv_freq[None, :]
    table_shape = (angles.shape[0],) + (1,) * (gradient.ndim - 2) + (half_dim,)
    cosine = jnp.cos(angles).reshape(table_shape)
    sine_table = jnp.sin(angles).reshape(table_shape)
    front_half = gradient[..., :half_dim]
    back_half = gradient[..., half_dim:]
    return jnp.concatenate([front_half * cosine + back_half * sine_table, back_half * cosine - front_half * sine_table], axis=-1)

def head_backward(operands):
    q_seq, k_seq, v_seq, d_seq, flag_value = operands
    group_len = TOK_DEV * GROUP_DEV
    half_len = group_len // 2
    n_groups = SEQ // group_len
    shifted = flag_value == 1

    def arrange(tensor):
        return jnp.where(shifted, jnp.roll(tensor, -half_len, axis=0), tensor)
    q_grp = arrange(q_seq).astype(jnp.float32).reshape(n_groups, group_len, -1, HEAD_WIDTH)
    d_grp = arrange(d_seq).astype(jnp.float32).reshape(n_groups, group_len, -1, HEAD_WIDTH)
    k_grp = arrange(k_seq).astype(jnp.float32).reshape(n_groups, group_len, HEAD_WIDTH)
    v_grp = arrange(v_seq).astype(jnp.float32).reshape(n_groups, group_len, HEAD_WIDTH)
    score_scale = 1.0 / math.sqrt(HEAD_WIDTH)
    causal = jnp.arange(group_len)[:, None] >= jnp.arange(group_len)[None, :]
    raw_score = jnp.einsum('nqgd,nkd->ngqk', q_grp, k_grp) * score_scale
    raw_score = jnp.where(causal, raw_score, -jnp.inf)
    log_total = jax.nn.logsumexp(raw_score, axis=-1, keepdims=True)
    probs = jnp.exp(raw_score - log_total)
    dprob = jnp.einsum('nqgd,nkd->ngqk', d_grp, v_grp)
    delta_row = lax.optimization_barrier(jnp.sum(probs * dprob, axis=-1, keepdims=True))
    dscore = probs * (dprob - delta_row)
    prob_low = lax.optimization_barrier(probs.astype(jnp.bfloat16)).astype(jnp.float32)
    dscore_low = lax.optimization_barrier(dscore.astype(jnp.bfloat16)).astype(jnp.float32)
    dq_grp = jnp.einsum('ngqk,nkd->nqgd', dscore_low, k_grp) * score_scale
    dk_grp = jnp.einsum('ngqk,nqgd->nkd', dscore_low, q_grp) * score_scale
    dv_grp = jnp.einsum('ngqk,nqgd->nkd', prob_low, d_grp)

    def restore(tensor):
        flat_rows = tensor.reshape((SEQ,) + tensor.shape[2:])
        return jnp.where(shifted, jnp.roll(flat_rows, half_len, axis=0), flat_rows)
    return (restore(dq_grp), restore(dk_grp), restore(dv_grp))

def reference(query, keys, values, out_grad, query_lowrank_state, value_lowrank_state, shift_flags):
    per_group = QUERY_HEADS_HALF // KEY_VALUE_HEADS

    def by_head(tensor, per_head):
        shaped = tensor.reshape((BATCH, SEQ, KEY_VALUE_HEADS) + per_head)
        return jnp.moveaxis(shaped, 2, 1).reshape((BATCH * KEY_VALUE_HEADS, SEQ) + per_head)

    def back_layout(tensor, per_head):
        shaped = tensor.reshape((BATCH, KEY_VALUE_HEADS, SEQ) + per_head)
        return jnp.moveaxis(shaped, 1, 2)
    flag_items = jnp.tile(shift_flags, BATCH).astype(jnp.int32)
    dq_all, dk_all, dv_all = lax.map(head_backward, (by_head(query, (per_group, HEAD_WIDTH)), by_head(keys, (HEAD_WIDTH,)), by_head(values, (HEAD_WIDTH,)), by_head(out_grad, (per_group, HEAD_WIDTH)), flag_items))
    positions = jnp.arange(SEQ, dtype=jnp.int32)
    dq_full = back_layout(dq_all, (per_group, HEAD_WIDTH))
    dk_full = back_layout(dk_all, (HEAD_WIDTH,))
    dv_full = back_layout(dv_all, (HEAD_WIDTH,))
    query_gradient = jax.vmap(lambda gradient: rope_back(gradient, positions))(dq_full).astype(jnp.bfloat16).reshape(BATCH, SEQ, QUERY_HEADS_HALF * HEAD_WIDTH)
    key_gradient = jax.vmap(lambda gradient: rope_back(gradient, positions))(dk_full).astype(jnp.bfloat16).reshape(BATCH, SEQ, KEY_VALUE_HEADS * HEAD_WIDTH)
    value_gradient = dv_full.astype(jnp.bfloat16).reshape(BATCH, SEQ, KEY_VALUE_HEADS * HEAD_WIDTH)
    query_adapter_gradient = ADAPTER_SCALE * jnp.dot(query_lowrank_state.reshape(-1, ADAPTER_RANK).T, query_gradient.reshape(-1, QUERY_HEADS_HALF * HEAD_WIDTH), preferred_element_type=jnp.float32)
    value_adapter_gradient = ADAPTER_SCALE * jnp.dot(value_lowrank_state.reshape(-1, ADAPTER_RANK).T, value_gradient.reshape(-1, KEY_VALUE_HEADS * HEAD_WIDTH), preferred_element_type=jnp.float32)
    return (query_gradient, key_gradient, value_gradient, query_adapter_gradient, value_adapter_gradient)
```

```python
import math

import jax
import jax.numpy as jnp
from jax import lax
from jax.experimental import pallas as pl
from jax.experimental.pallas import tpu as pltpu
from jax.sharding import PartitionSpec as P

QUERY_HEADS_HALF = 32
KEY_VALUE_HEADS = 4
HEAD_WIDTH = 128
GROUP_DEV = 8
TOK_DEV = 128
HALF_KV = KEY_VALUE_HEADS // 2
PER_GROUP = QUERY_HEADS_HALF // KEY_VALUE_HEADS
RANK = 8
CHIPS = GROUP_DEV // 2
PACK_ROWS = 4 * TOK_DEV + 16
Q_TILES = PER_GROUP // 2
ADAPTER_SCALE = 2.0
SCORE_SCALE = 1.0 / math.sqrt(HEAD_WIDTH)
EXP2_SCALE = SCORE_SCALE * math.log2(math.e)
MASKED = -1e30
NT = (((1,), (1,)), ((), ()))
TN = (((0,), (0,)), ((), ()))
VMEM_LIMIT = 56 * 1024 * 1024


def head_columns(ref, head):
    return ref[:, pl.ds(pl.multiple_of(head * HEAD_WIDTH, HEAD_WIDTH), HEAD_WIDTH)]


def pack_kernel(order_ref, keys_ref, values_ref, low_ref, plain_ref, moved_ref):
    for half, out in enumerate((plain_ref, moved_ref)):
        for sub in range(HALF_KV):
            head = order_ref[half * HALF_KV + sub]
            out[sub * TOK_DEV : (sub + 1) * TOK_DEV, :] = head_columns(keys_ref, head)
            out[(2 + sub) * TOK_DEV : (3 + sub) * TOK_DEV, :] = head_columns(values_ref, head)
        out[4 * TOK_DEV :, :] = low_ref[...]


def pack(order, keys, values, low_rows):
    whole = pl.BlockSpec(memory_space=pltpu.VMEM)
    shape = jax.ShapeDtypeStruct((PACK_ROWS, HEAD_WIDTH), jnp.bfloat16)
    return pl.pallas_call(
        pack_kernel,
        out_shape=(shape, shape),
        in_specs=[pl.BlockSpec(memory_space=pltpu.SMEM), whole, whole, whole],
        out_specs=(whole, whole),
        name="pack_heads",
    )(order, keys, values, low_rows)


def group_rows(x):
    return x.reshape(x.shape[0] // 8, 8, x.shape[1])


def attention_kernel(
    order_ref, count_ref, q_ref, d_ref, *refs
):
    mine = refs[:CHIPS]
    other = refs[CHIPS : 2 * CHIPS]
    cos_ref, sin_ref, low_ref = refs[2 * CHIPS : 2 * CHIPS + 3]
    refs = refs[2 * CHIPS + 3 :]
    refs = refs[len(refs) - 13 :]
    gq_ref, qad_ref, vad_ref, keep_ref, send_ref = refs[:5]
    s_ref, dp_ref, m_ref, l_ref, w_ref, dq_ref, dk_ref, dv_ref = refs[5:]
    sub = pl.program_id(0)
    tile = pl.program_id(1)
    chunks = count_ref[0]
    core = count_ref[1]
    rows = 2 * TOK_DEV
    q = jnp.concatenate([q_ref[:, :HEAD_WIDTH], q_ref[:, HEAD_WIDTH:]], axis=0)
    d = jnp.concatenate([d_ref[:, :HEAD_WIDTH], d_ref[:, HEAD_WIDTH:]], axis=0)
    k_rows = pl.ds(pl.multiple_of(sub * TOK_DEV, TOK_DEV), TOK_DEV)
    v_rows = pl.ds(pl.multiple_of((2 + sub) * TOK_DEV, TOK_DEV), TOK_DEV)

    def chunk(j, which):
        return jnp.concatenate([mine[j][which, :], other[j][which, :]], axis=0)

    def each_chunk(body):
        for j in range(CHIPS):
            if j == 0:
                body(j)
            else:
                pl.when(j < chunks)(lambda j=j: body(j))

    m_ref[...] = jnp.full_like(m_ref, MASKED)
    l_ref[...] = jnp.zeros_like(l_ref)
    w_ref[...] = jnp.zeros_like(w_ref)

    def scores(j):
        s = lax.dot_general(chunk(j, k_rows), q, NT, preferred_element_type=jnp.float32)
        if j == 0:
            key = lax.broadcasted_iota(jnp.int32, (rows, rows), 0)
            row = lax.broadcasted_iota(jnp.int32, (rows, rows), 1) % TOK_DEV
            limit = jnp.where(core == 1, rows, 0)
            allowed = (key <= row) | ((key >= TOK_DEV) & (key < limit))
            s = jnp.where(allowed, s, MASKED)
        s_ref[j] = s
        m_ref[...] = jnp.maximum(m_ref[...], jnp.max(group_rows(s), axis=0))
        dp_ref[j] = lax.dot_general(chunk(j, v_rows), d, NT, preferred_element_type=jnp.float32)

    each_chunk(scores)
    top = jnp.max(m_ref[...], axis=0, keepdims=True) * EXP2_SCALE

    def weights(j):
        p = jnp.exp2(s_ref[j] * EXP2_SCALE - top)
        s_ref[j] = p
        l_ref[...] += jnp.sum(group_rows(p), axis=0)
        w_ref[...] += jnp.sum(group_rows(p * dp_ref[j]), axis=0)

    each_chunk(weights)
    inverse = 1.0 / jnp.sum(l_ref[...], axis=0, keepdims=True)
    delta = jnp.sum(w_ref[...], axis=0, keepdims=True) * inverse

    def gradients(j):
        p = s_ref[j] * inverse
        ds = (p * (dp_ref[j] - delta)).astype(jnp.bfloat16)
        dv = jnp.dot(p.astype(jnp.bfloat16), d, preferred_element_type=jnp.float32)
        dk = jnp.dot(ds, q, preferred_element_type=jnp.float32)
        dq = lax.dot_general(ds, chunk(j, k_rows), TN, preferred_element_type=jnp.float32)
        if j == 0:
            dq_ref[...] = dq
        else:
            dq_ref[...] += dq

        @pl.when(tile == 0)
        def _():
            dk_ref[j] = dk
            dv_ref[j] = dv

        @pl.when(tile > 0)
        def _():
            dk_ref[j] += dk
            dv_ref[j] += dv

    each_chunk(gradients)
    dq = dq_ref[...] * SCORE_SCALE
    for h in range(2):
        x = dq[h * TOK_DEV : (h + 1) * TOK_DEV, :]
        turned = x * cos_ref[...] + pltpu.roll(x, HEAD_WIDTH // 2, 1) * sin_ref[...]
        low = turned.astype(jnp.bfloat16)
        gq_ref[:, h * HEAD_WIDTH : (h + 1) * HEAD_WIDTH] = low
        qad_ref[h] = (
            jnp.dot(low_ref[...], low, preferred_element_type=jnp.float32)[:RANK] * ADAPTER_SCALE
        )

    @pl.when(tile == Q_TILES - 1)
    def _():
        for j in range(CHIPS):

            @pl.when(j >= chunks)
            def _():
                dk_ref[j] = jnp.zeros(dk_ref.shape[1:], jnp.float32)
                dv_ref[j] = jnp.zeros(dv_ref.shape[1:], jnp.float32)

            keep_ref[j, k_rows, :] = dk_ref[j, :TOK_DEV]
            keep_ref[j, v_rows, :] = dv_ref[j, :TOK_DEV]
            send_ref[j, k_rows, :] = dk_ref[j, TOK_DEV:].astype(jnp.bfloat16)
            send_ref[j, v_rows, :] = dv_ref[j, TOK_DEV:].astype(jnp.bfloat16)
        vad_ref[0] = jnp.zeros(vad_ref.shape[1:], jnp.float32)
        for j in range(CHIPS):

            @pl.when(j < chunks)
            def _():
                term = jnp.zeros((16, HEAD_WIDTH), jnp.float32)
                for c, side in enumerate((mine, other)):
                    grad = dv_ref[j, c * TOK_DEV : (c + 1) * TOK_DEV].astype(jnp.bfloat16)
                    term += jnp.dot(
                        side[j][4 * TOK_DEV :, :], grad, preferred_element_type=jnp.float32
                    )
                vad_ref[0] += term[:RANK] * ADAPTER_SCALE


def attention(order, counts, query, out_grad, mine, other, cosine, sine, low_rows, before):
    tok = TOK_DEV
    pair = 2 * HEAD_WIDTH

    def whole(shape):
        return pl.BlockSpec(shape, lambda s, t, o, c: (0,) * len(shape))

    columns = pl.BlockSpec((tok, pair), lambda s, t, o, c: (0, o[s] * Q_TILES + t))
    in_specs = [columns, columns]
    in_specs += [whole((PACK_ROWS, HEAD_WIDTH))] * (2 * CHIPS)
    in_specs += [whole((tok, HEAD_WIDTH))] * 2 + [whole((16, HEAD_WIDTH))]
    operands = [query, out_grad, *mine, *other, cosine, sine, low_rows]
    aliases = {}
    if before is not None:
        for out, array in enumerate(before):
            aliases[2 + len(operands)] = out
            operands.append(array)
            in_specs.append(pl.BlockSpec(memory_space=pl.ANY))
    work = 8 * 2.5 * 10 * 2 * 256 * 256 * 128
    return pl.pallas_call(
        attention_kernel,
        grid_spec=pltpu.PrefetchScalarGridSpec(
            num_scalar_prefetch=2,
            grid=(HALF_KV, Q_TILES),
            in_specs=in_specs,
            out_specs=[
                columns,
                pl.BlockSpec((2, RANK, HEAD_WIDTH), lambda s, t, o, c: (o[s] * Q_TILES + t, 0, 0)),
                pl.BlockSpec((1, RANK, HEAD_WIDTH), lambda s, t, o, c: (s, 0, 0)),
                whole((CHIPS, 4 * tok, HEAD_WIDTH)),
                whole((CHIPS, 4 * tok, HEAD_WIDTH)),
            ],
            scratch_shapes=[
                pltpu.VMEM((CHIPS, 2 * tok, 2 * tok), jnp.float32),
                pltpu.VMEM((CHIPS, 2 * tok, 2 * tok), jnp.float32),
                pltpu.VMEM((8, 2 * tok), jnp.float32),
                pltpu.VMEM((8, 2 * tok), jnp.float32),
                pltpu.VMEM((8, 2 * tok), jnp.float32),
                pltpu.VMEM((2 * tok, HEAD_WIDTH), jnp.float32),
                pltpu.VMEM((CHIPS, 2 * tok, HEAD_WIDTH), jnp.float32),
                pltpu.VMEM((CHIPS, 2 * tok, HEAD_WIDTH), jnp.float32),
            ],
        ),
        out_shape=[
            jax.ShapeDtypeStruct((tok, QUERY_HEADS_HALF * HEAD_WIDTH), jnp.bfloat16),
            jax.ShapeDtypeStruct((QUERY_HEADS_HALF, RANK, HEAD_WIDTH), jnp.float32),
            jax.ShapeDtypeStruct((HALF_KV, RANK, HEAD_WIDTH), jnp.float32),
            jax.ShapeDtypeStruct((CHIPS, 4 * tok, HEAD_WIDTH), jnp.float32),
            jax.ShapeDtypeStruct((CHIPS, 4 * tok, HEAD_WIDTH), jnp.bfloat16),
        ],
        input_output_aliases=aliases,
        compiler_params=pltpu.CompilerParams(
            dimension_semantics=("arbitrary", "arbitrary"), vmem_limit_bytes=VMEM_LIMIT
        ),
        cost_estimate=pl.CostEstimate(
            flops=int(work), bytes_accessed=8 << 20, transcendentals=8 * 3 * 65536
        ),
        name="attention_plain" if before is None else "attention_moved",
    )(order, counts, *operands)


def finish_kernel(order_ref, cos_ref, sin_ref, *refs):
    gk_ref, gv_ref = refs[-2:]
    per_half = len(refs[:-2]) // 2
    for half in range(2):
        keep_ref, pair_ref, *arrived = refs[half * per_half : (half + 1) * per_half]
        total = keep_ref[0] + pair_ref[0].astype(jnp.float32)
        for part in arrived:
            total += part[...].astype(jnp.float32)
        for sub in range(HALF_KV):
            head = order_ref[half * HALF_KV + sub]
            columns = pl.ds(pl.multiple_of(head * HEAD_WIDTH, HEAD_WIDTH), HEAD_WIDTH)
            dk = total[sub * TOK_DEV : (sub + 1) * TOK_DEV] * SCORE_SCALE
            turned = dk * cos_ref[...] + pltpu.roll(dk, HEAD_WIDTH // 2, 1) * sin_ref[...]
            gk_ref[:, columns] = turned.astype(jnp.bfloat16)
            gv_ref[:, columns] = total[(2 + sub) * TOK_DEV : (3 + sub) * TOK_DEV].astype(
                jnp.bfloat16
            )


def finish(order, cosine, sine, halves):
    operands = []
    for keep, from_pair, arrived in halves:
        operands += [keep, from_pair, *arrived]
    whole = pl.BlockSpec(memory_space=pltpu.VMEM)
    shape = jax.ShapeDtypeStruct((TOK_DEV, KEY_VALUE_HEADS * HEAD_WIDTH), jnp.bfloat16)
    return pl.pallas_call(
        finish_kernel,
        out_shape=(shape, shape),
        in_specs=[pl.BlockSpec(memory_space=pltpu.SMEM)] + [whole] * (2 + len(operands)),
        out_specs=(whole, whole),
        compiler_params=pltpu.CompilerParams(vmem_limit_bytes=VMEM_LIMIT),
        name="finish_keys_values",
    )(order, cosine, sine, *operands)


def local(query, keys, values, out_grad, query_lowrank_state, value_lowrank_state, shift_flags):
    ctx_index = lax.axis_index("ctx")
    ctx_count = lax.axis_size("ctx")
    dp_count = lax.axis_size("dp")
    half_group = GROUP_DEV // 2
    core = ctx_index % 2
    pair = [(i, i ^ 1) for i in range(ctx_count)]
    chip_slots = (
        (ctx_index % GROUP_DEV) // 2,
        ((ctx_index + half_group) % GROUP_DEV) // 2,
    )

    def forward(distance, half):
        offset = half * half_group
        return [
            (i, (i + 2 * distance) % ctx_count)
            for i in range(ctx_count)
            if ((i + offset) % GROUP_DEV) // 2 + distance < CHIPS
        ]

    def backward(distance, half):
        return [(b, a) for a, b in forward(distance, half)]

    flags = shift_flags
    plain_rank = jnp.cumsum(1 - flags) - 1
    moved_rank = HALF_KV + jnp.cumsum(flags) - 1
    place = jnp.where(flags == 1, moved_rank, plain_rank)
    order = jnp.sum(
        jnp.where(
            place[None, :] == jnp.arange(KEY_VALUE_HEADS)[:, None],
            jnp.arange(KEY_VALUE_HEADS)[None, :],
            0,
        ),
        axis=1,
    ).astype(jnp.int32)

    def low_rows(state):
        return jnp.pad(state[0].T, ((0, 16 - RANK), (0, 0)))

    query_low = low_rows(query_lowrank_state)
    value_low = low_rows(value_lowrank_state)
    half_dim = HEAD_WIDTH // 2
    positions = ctx_index * TOK_DEV + jnp.arange(TOK_DEV, dtype=jnp.int32)
    inv_freq = 10000.0 ** (-(jnp.arange(half_dim, dtype=jnp.float32) * 2.0) / HEAD_WIDTH)
    angles = positions.astype(jnp.float32)[:, None] * inv_freq[None, :]
    cos_half, sin_half = jnp.cos(angles), jnp.sin(angles)
    cosine = jnp.concatenate([cos_half, cos_half], axis=1)
    sine = jnp.concatenate([sin_half, -sin_half], axis=1)

    packed = pack(order, keys[0], values[0], value_low)
    mine = [[packed[0]], [packed[1]]]
    other = [[], []]
    for half in range(2):
        for distance in range(1, CHIPS):
            mine[half].append(lax.ppermute(packed[half], "ctx", forward(distance, half)))
    both = lax.ppermute(jnp.stack([part for half in mine for part in half]), "ctx", pair)
    for half in range(2):
        other[half] = [both[half * CHIPS + j] for j in range(CHIPS)]

    results = []
    before = None
    for half in range(2):
        counts = jnp.stack([chip_slots[half] + 1, core]).astype(jnp.int32)
        result = attention(
            order[half * HALF_KV : (half + 1) * HALF_KV],
            counts,
            query[0],
            out_grad[0],
            mine[half],
            other[half],
            cosine,
            sine,
            query_low,
            before,
        )
        before = (result[0], result[1])
        results.append(result)
    gq, query_terms = before
    value_terms = jnp.concatenate([results[0][2], results[1][2]], axis=0)

    from_pair = lax.ppermute(jnp.concatenate([results[0][4], results[1][4]]), "ctx", pair)
    halves = []
    for half in range(2):
        keep = results[half][3]
        got = from_pair[half * CHIPS : (half + 1) * CHIPS]
        arrived = []
        for distance in range(1, CHIPS):
            part = (keep[distance] + got[distance].astype(jnp.float32)).astype(jnp.bfloat16)
            arrived.append(lax.ppermute(part, "ctx", backward(distance, half)))
        halves.append((keep[:1], got[:1], arrived))
    gk, gv = finish(order, cosine, sine, halves)

    value_rows = value_terms.reshape(ctx_count, 1, HEAD_WIDTH)
    terms = jnp.concatenate([query_terms, value_rows], axis=1)
    terms = jnp.sum(lax.all_to_all(terms, "ctx", 0, 0), axis=0)
    terms = jnp.sum(
        lax.all_to_all(jnp.broadcast_to(terms[None], (dp_count,) + terms.shape), "dp", 0, 0), axis=0
    )
    terms = lax.all_to_all(jnp.broadcast_to(terms[None], (ctx_count,) + terms.shape), "ctx", 0, 0)
    query_adapter = jnp.transpose(terms[:, :RANK], (1, 0, 2)).reshape(RANK, -1)
    value_heads = terms[:, RANK].reshape(KEY_VALUE_HEADS, RANK, HEAD_WIDTH)
    value_adapter = jnp.transpose(jnp.take(value_heads, place, axis=0), (1, 0, 2)).reshape(RANK, -1)
    return gq[None], gk[None], gv[None], query_adapter, value_adapter


def solution(mesh):
    rows = P("dp", "ctx", None)
    return jax.shard_map(
        local,
        mesh=mesh,
        in_specs=(rows,) * 6 + (P(),),
        out_specs=(rows, rows, rows, P(), P()),
        check_vma=False,
    )
```

```python
import math

import jax
import jax.numpy as jnp
from jax import lax
from jax.experimental import pallas as pl
from jax.experimental.pallas import tpu as pltpu
from jax.sharding import Mesh, PartitionSpec as P

QUERY_HEADS_HALF = 32
KEY_VALUE_HEADS = 4
HEAD_WIDTH = 128
GROUP_DEV = 8
TOK_DEV = 128
HALF_KV = KEY_VALUE_HEADS // 2
PER_GROUP = QUERY_HEADS_HALF // KEY_VALUE_HEADS
RANK = 8
CHIPS = GROUP_DEV // 2
PACK_ROWS = 4 * TOK_DEV + 16
PEERS = 16
TERM_ROWS = 32
TERM_BLOCK = PEERS // KEY_VALUE_HEADS
ADAPTER_SCALE = 2.0
SCORE_SCALE = 1.0 / math.sqrt(HEAD_WIDTH)
EXP2_SCALE = SCORE_SCALE * math.log2(math.e)
MASKED = -1e30
NT = (((1,), (1,)), ((), ()))
TN = (((0,), (0,)), ((), ()))
VMEM_LIMIT = 56 * 1024 * 1024
SEQ_AXES = ("yh", "zc")
SUM_AXES = ("dp", "yh")


def head_of(flags, half, sub):
    hit = [flags[head] == half for head in range(KEY_VALUE_HEADS)]
    low = jnp.where(hit[0], 0, jnp.where(hit[1], 1, 2))
    high = jnp.where(hit[3], 3, jnp.where(hit[2], 2, 1))
    return jnp.where(sub == 0, low, high)


def columns_of(head):
    return pl.ds(pl.multiple_of(head * HEAD_WIDTH, HEAD_WIDTH), HEAD_WIDTH)


def pack_kernel(flags_ref, keys_ref, values_ref, low_ref, plain_ref, moved_ref):
    eye = (
        lax.broadcasted_iota(jnp.int32, (TOK_DEV, TOK_DEV), 0)
        == lax.broadcasted_iota(jnp.int32, (TOK_DEV, TOK_DEV), 1)
    ).astype(jnp.bfloat16)
    low = lax.dot_general(low_ref[...], eye, TN, preferred_element_type=jnp.float32)
    low = jnp.concatenate([low, jnp.zeros_like(low)], axis=0).astype(jnp.bfloat16)
    for half, out in enumerate((plain_ref, moved_ref)):
        for sub in range(HALF_KV):
            columns = columns_of(head_of(flags_ref, half, sub))
            out[sub * TOK_DEV : (sub + 1) * TOK_DEV, :] = keys_ref[:, columns]
            out[(2 + sub) * TOK_DEV : (3 + sub) * TOK_DEV, :] = values_ref[:, columns]
        out[4 * TOK_DEV :, :] = low


def pack(flags, keys, values, low):
    whole = pl.BlockSpec(memory_space=pltpu.VMEM)
    shape = jax.ShapeDtypeStruct((PACK_ROWS, HEAD_WIDTH), jnp.bfloat16)
    return pl.pallas_call(
        pack_kernel,
        out_shape=(shape, shape),
        in_specs=[pl.BlockSpec(memory_space=pltpu.SMEM), whole, whole, whole],
        out_specs=(whole, whole),
        name="pack_heads",
    )(flags, keys, values, low)


def attention_kernel(flags_ref, table_ref, q_ref, d_ref, mine_ref, other_ref, *refs):
    cos_ref, sin_ref, low_ref = refs[:3]
    refs = refs[len(refs) - 9 :]
    gq_ref, term_ref, keep_ref, send_ref = refs[:4]
    k_all, v_all, low_all, dk_ref, dv_ref = refs[4:]
    sub = pl.program_id(0)
    chunks = table_ref[0]
    core = table_ref[1]
    rows = 2 * TOK_DEV
    wide = PER_GROUP * TOK_DEV
    k_rows = pl.ds(pl.multiple_of(sub * TOK_DEV, TOK_DEV), TOK_DEV)
    v_rows = pl.ds(pl.multiple_of((2 + sub) * TOK_DEV, TOK_DEV), TOK_DEV)

    def branch(n):
        for j in range(n):
            place = table_ref[2 + j]
            for c, side in enumerate((mine_ref, other_ref)):
                span = slice(j * rows + c * TOK_DEV, j * rows + (c + 1) * TOK_DEV)
                k_all[span, :] = side[place, k_rows, :]
                v_all[span, :] = side[place, v_rows, :]
                low_all[:, span] = side[place, 4 * TOK_DEV :, :]
        width = n * rows
        key = lax.broadcasted_iota(jnp.int32, (rows, wide), 0)
        row = lax.broadcasted_iota(jnp.int32, (rows, wide), 1) % TOK_DEV
        limit = jnp.where(core == 1, rows, 0)
        allowed = (key <= row) | ((key >= TOK_DEV) & (key < limit))

        def stacked(ref):
            return jnp.concatenate(
                [ref[:, h * HEAD_WIDTH : (h + 1) * HEAD_WIDTH] for h in range(PER_GROUP)], axis=0
            )

        q = stacked(q_ref)
        d = stacked(d_ref)
        k = k_all[:width, :]
        s = lax.dot_general(k, q, NT, preferred_element_type=jnp.float32)
        near = jnp.where(allowed, s[:rows], MASKED)
        s = near if n == 1 else jnp.concatenate([near, s[rows:]], axis=0)
        dp = lax.dot_general(v_all[:width, :], d, NT, preferred_element_type=jnp.float32)
        top = jnp.max(s, axis=0, keepdims=True) * EXP2_SCALE
        p = jnp.exp2(s * EXP2_SCALE - top)
        inverse = 1.0 / jnp.sum(p, axis=0, keepdims=True)
        delta = jnp.sum(p * dp, axis=0, keepdims=True) * inverse
        p = p * inverse
        ds = (p * (dp - delta)).astype(jnp.bfloat16)
        dv_ref[:width, :] = jnp.dot(p.astype(jnp.bfloat16), d, preferred_element_type=jnp.float32)
        dk_ref[:width, :] = jnp.dot(ds, q, preferred_element_type=jnp.float32)
        dq = lax.dot_general(ds, k, TN, preferred_element_type=jnp.float32) * SCORE_SCALE
        low_rank = low_ref[...]
        parts = []
        for h in range(PER_GROUP):
            x = dq[h * TOK_DEV : (h + 1) * TOK_DEV, :]
            turned = x * cos_ref[...] + pltpu.roll(x, HEAD_WIDTH // 2, 1) * sin_ref[...]
            low = turned.astype(jnp.bfloat16)
            gq_ref[:, h * HEAD_WIDTH : (h + 1) * HEAD_WIDTH] = low
            parts.append(
                lax.dot_general(low_rank, low, TN, preferred_element_type=jnp.float32)
                * ADAPTER_SCALE
            )
        value_part = (
            jnp.dot(
                low_all[:, :width],
                dv_ref[:width, :].astype(jnp.bfloat16),
                preferred_element_type=jnp.float32,
            )
            * ADAPTER_SCALE
        )
        pair_rows = 2 * RANK // PER_GROUP
        blank = jnp.zeros((2 * RANK - pair_rows, HEAD_WIDTH), jnp.float32)
        for i in range(TERM_BLOCK):
            block = jnp.concatenate(parts[2 * i : 2 * i + 2], axis=0)
            term_ref[i, : 2 * RANK, :] = block.astype(jnp.bfloat16)
            block = jnp.concatenate([value_part[i * pair_rows : (i + 1) * pair_rows], blank], axis=0)
            term_ref[i, 2 * RANK :, :] = block.astype(jnp.bfloat16)
        for j in range(CHIPS):
            place = table_ref[2 + j]
            if j < n:
                span = slice(j * rows, j * rows + TOK_DEV)
                past = slice(j * rows + TOK_DEV, (j + 1) * rows)
                keep_ref[place, k_rows, :] = dk_ref[span, :]
                keep_ref[place, v_rows, :] = dv_ref[span, :]
                send_ref[place, k_rows, :] = dk_ref[past, :].astype(jnp.bfloat16)
                send_ref[place, v_rows, :] = dv_ref[past, :].astype(jnp.bfloat16)
            else:
                keep_ref[place, k_rows, :] = jnp.zeros((TOK_DEV, HEAD_WIDTH), jnp.float32)
                keep_ref[place, v_rows, :] = jnp.zeros((TOK_DEV, HEAD_WIDTH), jnp.float32)
                send_ref[place, k_rows, :] = jnp.zeros((TOK_DEV, HEAD_WIDTH), jnp.bfloat16)
                send_ref[place, v_rows, :] = jnp.zeros((TOK_DEV, HEAD_WIDTH), jnp.bfloat16)

    for n in range(1, CHIPS + 1):
        pl.when(chunks == n)(lambda n=n: branch(n))


def attention(half, flags, table, query, out_grad, mine, other, cosine, sine, low, before):
    tok = TOK_DEV
    wide = PER_GROUP * HEAD_WIDTH
    keys = CHIPS * 2 * tok

    def whole(shape):
        return pl.BlockSpec(shape, lambda s, f, t: (0,) * len(shape))

    columns = pl.BlockSpec((tok, wide), lambda s, f, t: (0, head_of(f, half, s)))
    terms = pl.BlockSpec(
        (TERM_BLOCK, TERM_ROWS, HEAD_WIDTH), lambda s, f, t: (head_of(f, half, s), 0, 0)
    )
    stack = whole((CHIPS, PACK_ROWS, HEAD_WIDTH))
    grads = whole((CHIPS, 4 * tok, HEAD_WIDTH))
    table_spec = whole((tok, HEAD_WIDTH))
    in_specs = [columns, columns, stack, stack, table_spec, table_spec, whole((tok, RANK))]
    operands = [query, out_grad, mine, other, cosine, sine, low]
    aliases = {}
    if before is not None:
        for out, array in enumerate(before):
            aliases[2 + len(operands)] = out
            operands.append(array)
            in_specs.append(pl.BlockSpec(memory_space=pl.ANY))
    return pl.pallas_call(
        attention_kernel,
        grid_spec=pltpu.PrefetchScalarGridSpec(
            num_scalar_prefetch=2,
            grid=(HALF_KV,),
            in_specs=in_specs,
            out_specs=[columns, terms, grads, grads],
            scratch_shapes=[
                pltpu.VMEM((keys, HEAD_WIDTH), jnp.bfloat16),
                pltpu.VMEM((keys, HEAD_WIDTH), jnp.bfloat16),
                pltpu.VMEM((16, keys), jnp.bfloat16),
                pltpu.VMEM((keys, HEAD_WIDTH), jnp.float32),
                pltpu.VMEM((keys, HEAD_WIDTH), jnp.float32),
            ],
        ),
        out_shape=[
            jax.ShapeDtypeStruct((tok, QUERY_HEADS_HALF * HEAD_WIDTH), jnp.bfloat16),
            jax.ShapeDtypeStruct((PEERS, TERM_ROWS, HEAD_WIDTH), jnp.bfloat16),
            jax.ShapeDtypeStruct((CHIPS, 4 * tok, HEAD_WIDTH), jnp.float32),
            jax.ShapeDtypeStruct((CHIPS, 4 * tok, HEAD_WIDTH), jnp.bfloat16),
        ],
        input_output_aliases=aliases,
        compiler_params=pltpu.CompilerParams(
            dimension_semantics=("arbitrary",), vmem_limit_bytes=VMEM_LIMIT
        ),
        cost_estimate=pl.CostEstimate(
            flops=10 * HALF_KV * wide * keys * HEAD_WIDTH,
            bytes_accessed=6 << 20,
            transcendentals=HALF_KV * wide * keys,
        ),
        name="attention_plain" if half == 0 else "attention_moved",
    )(flags, table, *operands)


def finish_kernel(flags_ref, cos_ref, sin_ref, *refs):
    gk_ref, gv_ref = refs[-2:]
    start = 0
    for half, count in ((0, 1 + CHIPS), (1, 4)):
        keep_ref, pair_ref, *arrived = refs[start : start + count]
        start += count
        total = keep_ref[0] + pair_ref[0].astype(jnp.float32)
        for part in arrived:
            total += part[...].astype(jnp.float32)
        for sub in range(HALF_KV):
            columns = columns_of(head_of(flags_ref, half, sub))
            dk = total[sub * TOK_DEV : (sub + 1) * TOK_DEV] * SCORE_SCALE
            turned = dk * cos_ref[...] + pltpu.roll(dk, HEAD_WIDTH // 2, 1) * sin_ref[...]
            gk_ref[:, columns] = turned.astype(jnp.bfloat16)
            dv = total[(2 + sub) * TOK_DEV : (3 + sub) * TOK_DEV]
            gv_ref[:, columns] = dv.astype(jnp.bfloat16)


def finish(flags, cosine, sine, halves):
    tok = TOK_DEV

    def whole(shape):
        return pl.BlockSpec(shape, lambda i, f: (0,) * len(shape))

    first = whole((1, 4 * tok, HEAD_WIDTH))
    part = whole((4 * tok, HEAD_WIDTH))
    operands, in_specs = [cosine, sine], [whole((tok, HEAD_WIDTH))] * 2
    for keep, from_pair, arrived in halves:
        operands += [keep, from_pair, *arrived]
        in_specs += [first, first] + [part] * len(arrived)
    shape = jax.ShapeDtypeStruct((tok, KEY_VALUE_HEADS * HEAD_WIDTH), jnp.bfloat16)
    return pl.pallas_call(
        finish_kernel,
        grid_spec=pltpu.PrefetchScalarGridSpec(
            num_scalar_prefetch=1,
            grid=(1,),
            in_specs=in_specs,
            out_specs=[whole(shape.shape)] * 2,
        ),
        out_shape=[shape, shape],
        compiler_params=pltpu.CompilerParams(vmem_limit_bytes=VMEM_LIMIT),
        name="finish_keys_values",
    )(flags, *operands)


def exchange(array, axes):
    return lax.all_to_all(array, axes, 0, 0)


def to_all(array, axes):
    count = lax.axis_size(axes)
    return exchange(jnp.broadcast_to(array[None], (count,) + array.shape), axes)


def add_up(array):
    return jnp.sum(array.astype(jnp.float32), axis=0).astype(jnp.bfloat16)


def local(query, keys, values, out_grad, query_lowrank_state, value_lowrank_state, shift_flags):
    ctx_index = lax.axis_index(SEQ_AXES)
    ctx_count = lax.axis_size(SEQ_AXES)
    half_group = GROUP_DEV // 2
    core = ctx_index % 2
    slots = [((ctx_index + half * half_group) % GROUP_DEV) // 2 for half in range(2)]

    def send(array, pairs):
        return lax.ppermute(array, SEQ_AXES, pairs)

    def hop(distance, half, from_slots):
        return [
            (i, (i + 2 * distance) % ctx_count)
            for i in range(ctx_count)
            if ((i + half * half_group) % GROUP_DEV) // 2 in from_slots
        ]

    def back(pairs):
        return [(b, a) for a, b in pairs]

    pair = [(i, i ^ 1) for i in range(ctx_count)]
    plain_hops = [hop(n, 0, range(CHIPS - n)) for n in range(1, CHIPS)]
    side = hop(1, 1, (0, 2))
    cross = hop(2, 1, (0, 1))
    swap = hop(1, 1, (2,)) + hop(-1, 1, (3,))

    half_dim = HEAD_WIDTH // 2
    positions = ctx_index * TOK_DEV + jnp.arange(TOK_DEV, dtype=jnp.int32)
    inv_freq = 10000.0 ** (-(jnp.arange(half_dim, dtype=jnp.float32) * 2.0) / HEAD_WIDTH)
    angles = positions.astype(jnp.float32)[:, None] * inv_freq[None, :]
    cos_half, sin_half = jnp.cos(angles), jnp.sin(angles)
    cosine = jnp.concatenate([cos_half, cos_half], axis=1)
    sine = jnp.concatenate([sin_half, -sin_half], axis=1)
    late = (slots[1] == 2).astype(jnp.int32)
    plain_table = jnp.stack([slots[0] + 1, core] + [0, 1, 2, 3]).astype(jnp.int32)
    moved_table = jnp.stack(
        [slots[1] + 1, core, 0, 1 + late, 2 + late, 3 - 2 * late]
    ).astype(jnp.int32)

    plain, moved = pack(shift_flags, keys[0], values[0], value_lowrank_state[0])
    moved_cross = send(moved, cross)
    moved_side = send(moved, side)
    plain_got = [send(plain, pairs) for pairs in plain_hops]
    plain_got, cosine, sine, plain_table, moved_table = lax.optimization_barrier(
        (plain_got, cosine, sine, plain_table, moved_table)
    )
    plain_mine = jnp.stack([plain, *plain_got])
    plain_other = send(plain_mine, pair)
    low = query_lowrank_state[0]
    gq, terms, plain_keep, plain_send = attention(
        0, shift_flags, plain_table, query[0], out_grad[0], plain_mine, plain_other,
        cosine, sine, low, None,
    )
    moved_swap = send(moved_cross, swap)
    moved_mine = jnp.stack([moved, moved_side, moved_cross, moved_swap])
    moved_other = send(moved_mine, pair)
    plain_from = send(plain_send, pair)
    moved_other, plain_from = lax.optimization_barrier((moved_other, plain_from))
    plain_back = []
    for n in range(1, CHIPS):
        part = (plain_keep[n] + plain_from[n].astype(jnp.float32)).astype(jnp.bfloat16)
        plain_back.append(send(part, back(plain_hops[n - 1])))
    gq, terms, moved_keep, moved_send = attention(
        1, shift_flags, moved_table, query[0], out_grad[0], moved_mine, moved_other,
        cosine, sine, low, (gq, terms),
    )

    moved_from = send(moved_send, pair)
    terms = exchange(terms, "zc")
    terms, moved_from, plain_back = lax.optimization_barrier((terms, moved_from, plain_back))
    terms = add_up(terms)

    def partial(n):
        return moved_keep[n] + moved_from[n].astype(jnp.float32)

    side_back = send(partial(1).astype(jnp.bfloat16), back(side))
    swap_back = send(partial(3).astype(jnp.bfloat16), swap)
    terms = to_all(terms, SUM_AXES)
    terms, side_back, swap_back = lax.optimization_barrier((terms, side_back, swap_back))
    terms = add_up(terms)
    cross_part = (partial(2) + swap_back.astype(jnp.float32)).astype(jnp.bfloat16)
    cross_back = send(cross_part, back(cross))
    terms = to_all(terms, "zc")
    gk, gv = finish(
        shift_flags, cosine, sine,
        [(plain_keep, plain_from, plain_back), (moved_keep, moved_from, [side_back, cross_back])],
    )

    query_terms = terms[:, : 2 * RANK].reshape(QUERY_HEADS_HALF, RANK, HEAD_WIDTH)
    pair_rows = 2 * RANK // PER_GROUP
    value_terms = terms[:, 2 * RANK : 2 * RANK + pair_rows].reshape(
        KEY_VALUE_HEADS, RANK, HEAD_WIDTH
    )

    def wide(heads):
        return jnp.transpose(heads, (1, 0, 2)).reshape(RANK, -1).astype(jnp.float32)

    return gq[None], gk[None], gv[None], wide(query_terms), wide(value_terms)


def solution(mesh):
    dp, ctx = mesh.shape["dp"], mesh.shape["ctx"]
    split = Mesh(mesh.devices.reshape(dp, ctx // PEERS, PEERS), ("dp", "yh", "zc"))
    rows = P("dp", SEQ_AXES, None)
    return jax.shard_map(
        local,
        mesh=split,
        in_specs=(rows,) * 6 + (P(),),
        out_specs=(rows, rows, rows, P(), P()),
        check_vma=False,
    )
```

```python
from functools import partial
import math

import jax
import jax.numpy as jnp
from jax import lax
from jax.experimental import pallas as pl
from jax.experimental.pallas import tpu as pltpu
from jax.sharding import Mesh, PartitionSpec as P

QUERY_HEADS_HALF = 32
KEY_VALUE_HEADS = 4
HEAD_WIDTH = 128
GROUP_DEV = 8
TOK_DEV = 128
HALF_KV = KEY_VALUE_HEADS // 2
PER_GROUP = QUERY_HEADS_HALF // KEY_VALUE_HEADS
RANK = 8
PACK_ROWS = 4 * TOK_DEV + 16
PEERS = 16
TERM_ROWS = 32
TERM_BLOCK = PEERS // KEY_VALUE_HEADS
ADAPTER_SCALE = 2.0
SCORE_SCALE = 1.0 / math.sqrt(HEAD_WIDTH)
EXP2_SCALE = SCORE_SCALE * math.log2(math.e)
MASKED = -1e30
NT = (((1,), (1,)), ((), ()))
TN = (((0,), (0,)), ((), ()))
VMEM_LIMIT = 56 * 1024 * 1024
SEQ_AXES = ("yh", "zc")
SUM_AXES = ("dp", "yh")


def head_of(flags, half, sub):
    hit = [flags[head] == half for head in range(KEY_VALUE_HEADS)]
    low = jnp.where(hit[0], 0, jnp.where(hit[1], 1, 2))
    high = jnp.where(hit[3], 3, jnp.where(hit[2], 2, 1))
    return jnp.where(sub == 0, low, high)


def columns_of(head):
    return pl.ds(pl.multiple_of(head * HEAD_WIDTH, HEAD_WIDTH), HEAD_WIDTH)


def pack_kernel(flags_ref, table_ref, keys_ref, values_ref, low_ref, both_ref, light_ref):
    low = low_ref[...].astype(jnp.float32)
    low = jnp.concatenate([low, jnp.zeros_like(low)], axis=0).astype(jnp.bfloat16)
    for place in range(2):
        half = table_ref[2 + place]
        for sub in range(HALF_KV):
            columns = columns_of(head_of(flags_ref, half, sub))
            for kind, ref in enumerate((keys_ref, values_ref)):
                rows = slice((2 * kind + sub) * TOK_DEV, (2 * kind + sub + 1) * TOK_DEV)
                both_ref[place, rows, :] = ref[:, columns]
                if place == 0:
                    light_ref[rows, :] = ref[:, columns]
        both_ref[place, 4 * TOK_DEV :, :] = low
    light_ref[4 * TOK_DEV :, :] = low


def pack(flags, table, keys, values, low):
    whole = pl.BlockSpec(memory_space=pltpu.VMEM)
    scalars = pl.BlockSpec(memory_space=pltpu.SMEM)
    return pl.pallas_call(
        pack_kernel,
        out_shape=(
            jax.ShapeDtypeStruct((2, PACK_ROWS, HEAD_WIDTH), jnp.bfloat16),
            jax.ShapeDtypeStruct((PACK_ROWS, HEAD_WIDTH), jnp.bfloat16),
        ),
        in_specs=[scalars, scalars, whole, whole, whole],
        out_specs=(whole, whole),
        name="pack_heads",
    )(flags, table, keys, values, low)


def attention_kernel(heavy, flags_ref, table_ref, q_ref, d_ref, *refs):
    chunks = 4 if heavy else 2
    mine, other = refs[:chunks], refs[chunks : 2 * chunks]
    cos_ref, sin_ref, low_ref = refs[2 * chunks : 2 * chunks + 3]
    outs = refs[len(refs) - (11 if heavy else 9) : len(refs) - 5]
    gq_ref, term_ref, keep_ref, send_ref, *swap_refs = outs
    k_all, v_all, low_all, dk_ref, dv_ref = refs[len(refs) - 5 :]
    sub = pl.program_id(0)
    odd, core = table_ref[0], table_ref[1]
    rows = 2 * TOK_DEV
    wide = PER_GROUP * TOK_DEV
    k_rows = pl.ds(pl.multiple_of(sub * TOK_DEV, TOK_DEV), TOK_DEV)
    v_rows = pl.ds(pl.multiple_of((2 + sub) * TOK_DEV, TOK_DEV), TOK_DEV)

    def branch(n):
        for j in range(n):
            for c, side in enumerate((mine[j], other[j])):
                span = slice(j * rows + c * TOK_DEV, j * rows + (c + 1) * TOK_DEV)
                k_all[span, :] = side[0, k_rows, :]
                v_all[span, :] = side[0, v_rows, :]
                low_all[:, span] = side[0, 4 * TOK_DEV :, :]
        width = n * rows
        key = lax.broadcasted_iota(jnp.int32, (rows, wide), 0)
        row = lax.broadcasted_iota(jnp.int32, (rows, wide), 1) % TOK_DEV
        limit = jnp.where(core == 1, rows, 0)
        allowed = (key <= row) | ((key >= TOK_DEV) & (key < limit))

        def stacked(ref):
            return jnp.concatenate(
                [ref[:, h * HEAD_WIDTH : (h + 1) * HEAD_WIDTH] for h in range(PER_GROUP)], axis=0
            )

        q = stacked(q_ref)
        d = stacked(d_ref)
        k = k_all[:width, :]
        s = lax.dot_general(k, q, NT, preferred_element_type=jnp.float32)
        near = jnp.where(allowed, s[:rows], MASKED)
        s = near if n == 1 else jnp.concatenate([near, s[rows:]], axis=0)
        dp = lax.dot_general(v_all[:width, :], d, NT, preferred_element_type=jnp.float32)
        top = jnp.max(s, axis=0, keepdims=True) * EXP2_SCALE
        p = jnp.exp2(s * EXP2_SCALE - top)
        inverse = 1.0 / jnp.sum(p, axis=0, keepdims=True)
        delta = jnp.sum(p * dp, axis=0, keepdims=True) * inverse
        p = p * inverse
        ds = (p * (dp - delta)).astype(jnp.bfloat16)
        dv_ref[:width, :] = jnp.dot(p.astype(jnp.bfloat16), d, preferred_element_type=jnp.float32)
        dk_ref[:width, :] = jnp.dot(ds, q, preferred_element_type=jnp.float32)
        dq = lax.dot_general(ds, k, TN, preferred_element_type=jnp.float32) * SCORE_SCALE
        low_rank = low_ref[...]
        parts = []
        for h in range(PER_GROUP):
            x = dq[h * TOK_DEV : (h + 1) * TOK_DEV, :]
            turned = x * cos_ref[...] + pltpu.roll(x, HEAD_WIDTH // 2, 1) * sin_ref[...]
            low = turned.astype(jnp.bfloat16)
            gq_ref[:, h * HEAD_WIDTH : (h + 1) * HEAD_WIDTH] = low
            parts.append(
                jnp.dot(low_rank, low, preferred_element_type=jnp.float32) * ADAPTER_SCALE
            )
        value_part = (
            jnp.dot(
                low_all[:, :width],
                dv_ref[:width, :].astype(jnp.bfloat16),
                preferred_element_type=jnp.float32,
            )
            * ADAPTER_SCALE
        )
        pair_rows = 2 * RANK // PER_GROUP
        blank = jnp.zeros((2 * RANK - pair_rows, HEAD_WIDTH), jnp.float32)
        for i in range(TERM_BLOCK):
            block = jnp.concatenate(parts[2 * i : 2 * i + 2], axis=0)
            term_ref[i, : 2 * RANK, :] = block.astype(jnp.bfloat16)
            block = jnp.concatenate([value_part[i * pair_rows : (i + 1) * pair_rows], blank], axis=0)
            term_ref[i, 2 * RANK :, :] = block.astype(jnp.bfloat16)

        def store(ref, j, span):
            for grad_ref, to_rows in ((dk_ref, k_rows), (dv_ref, v_rows)):
                if j < n:
                    grad = grad_ref[j * rows + span * TOK_DEV : j * rows + (span + 1) * TOK_DEV, :]
                else:
                    grad = jnp.zeros((TOK_DEV, HEAD_WIDTH), jnp.float32)
                ref[to_rows, :] = grad.astype(ref.dtype)

        kept = (0, 1, 3) if heavy else (0, 1)
        for to, j in enumerate(kept):
            store(keep_ref.at[to], j, 0)
            store(send_ref.at[to], j, 1)
        for span, ref in enumerate(swap_refs):
            store(ref, 2, span)

    base = 3 if heavy else 1
    for more in range(2):
        pl.when(odd == more)(lambda n=base + more: branch(n))


def attention(heavy, flags, table, query, out_grad, mine, other, cosine, sine, low, before):
    tok = TOK_DEV
    wide = PER_GROUP * HEAD_WIDTH
    chunks = len(mine)
    keys = chunks * 2 * tok
    kept = chunks - 1 if heavy else chunks
    place = 1 if heavy else 0

    def whole(shape):
        return pl.BlockSpec(shape, lambda s, f, t: (0,) * len(shape))

    def head(f, t, s):
        return head_of(f, t[2 + place], s)

    columns = pl.BlockSpec((tok, wide), lambda s, f, t: (0, head(f, t, s)))
    terms = pl.BlockSpec((TERM_BLOCK, TERM_ROWS, HEAD_WIDTH), lambda s, f, t: (head(f, t, s), 0, 0))
    table_spec = whole((tok, HEAD_WIDTH))
    in_specs = [columns, columns]
    for array in (*mine, *other):
        at = place if array.shape[0] == 2 else 0
        in_specs.append(
            pl.BlockSpec((1, PACK_ROWS, HEAD_WIDTH), lambda s, f, t, at=at: (at, 0, 0))
        )
    in_specs += [table_spec, table_spec, whole((RANK, tok))]
    operands = [query, out_grad, *mine, *other, cosine, sine, low]
    aliases = {}
    if before is not None:
        for out, array in enumerate(before):
            aliases[2 + len(operands)] = out
            operands.append(array)
            in_specs.append(pl.BlockSpec(memory_space=pl.ANY))
    out_shape = [
        jax.ShapeDtypeStruct((tok, QUERY_HEADS_HALF * HEAD_WIDTH), jnp.bfloat16),
        jax.ShapeDtypeStruct((PEERS, TERM_ROWS, HEAD_WIDTH), jnp.bfloat16),
        jax.ShapeDtypeStruct((kept, 4 * tok, HEAD_WIDTH), jnp.float32),
        jax.ShapeDtypeStruct((kept, 4 * tok, HEAD_WIDTH), jnp.bfloat16),
    ]
    if heavy:
        out_shape += [jax.ShapeDtypeStruct((4 * tok, HEAD_WIDTH), jnp.bfloat16)] * 2
    return pl.pallas_call(
        partial(attention_kernel, heavy),
        grid_spec=pltpu.PrefetchScalarGridSpec(
            num_scalar_prefetch=2,
            grid=(HALF_KV,),
            in_specs=in_specs,
            out_specs=[columns, terms] + [whole(o.shape) for o in out_shape[2:]],
            scratch_shapes=[
                pltpu.VMEM((keys, HEAD_WIDTH), jnp.bfloat16),
                pltpu.VMEM((keys, HEAD_WIDTH), jnp.bfloat16),
                pltpu.VMEM((16, keys), jnp.bfloat16),
                pltpu.VMEM((keys, HEAD_WIDTH), jnp.float32),
                pltpu.VMEM((keys, HEAD_WIDTH), jnp.float32),
            ],
        ),
        out_shape=out_shape,
        input_output_aliases=aliases,
        compiler_params=pltpu.CompilerParams(
            dimension_semantics=("arbitrary",), vmem_limit_bytes=VMEM_LIMIT
        ),
        cost_estimate=pl.CostEstimate(
            flops=10 * HALF_KV * wide * keys * HEAD_WIDTH,
            bytes_accessed=6 << 20,
            transcendentals=HALF_KV * wide * keys,
        ),
        name="attention_heavy" if heavy else "attention_light",
    )(flags, table, *operands)


def finish_kernel(flags_ref, table_ref, cos_ref, sin_ref, *refs):
    light_keep, light_from, heavy_keep, heavy_from, side_ref, cross_ref, gk_ref, gv_ref = refs
    for place, (keep_ref, from_ref) in enumerate(
        ((light_keep, light_from), (heavy_keep, heavy_from))
    ):
        total = keep_ref[0] + from_ref[0].astype(jnp.float32) + side_ref[place].astype(jnp.float32)
        if place == 0:
            total += cross_ref[...].astype(jnp.float32)
        for sub in range(HALF_KV):
            columns = columns_of(head_of(flags_ref, table_ref[2 + place], sub))
            dk = total[sub * TOK_DEV : (sub + 1) * TOK_DEV] * SCORE_SCALE
            turned = dk * cos_ref[...] + pltpu.roll(dk, HEAD_WIDTH // 2, 1) * sin_ref[...]
            gk_ref[:, columns] = turned.astype(jnp.bfloat16)
            dv = total[(2 + sub) * TOK_DEV : (3 + sub) * TOK_DEV]
            gv_ref[:, columns] = dv.astype(jnp.bfloat16)


def finish(flags, table, cosine, sine, kept, side_back, cross_back):
    tok = TOK_DEV

    def whole(shape):
        return pl.BlockSpec(shape, lambda i, f, t: (0,) * len(shape))

    first = whole((1, 4 * tok, HEAD_WIDTH))
    shape = jax.ShapeDtypeStruct((tok, KEY_VALUE_HEADS * HEAD_WIDTH), jnp.bfloat16)
    return pl.pallas_call(
        finish_kernel,
        grid_spec=pltpu.PrefetchScalarGridSpec(
            num_scalar_prefetch=2,
            grid=(1,),
            in_specs=[whole((tok, HEAD_WIDTH))] * 2
            + [first] * 4
            + [whole(side_back.shape), whole(cross_back.shape)],
            out_specs=[whole(shape.shape)] * 2,
        ),
        out_shape=[shape, shape],
        compiler_params=pltpu.CompilerParams(vmem_limit_bytes=VMEM_LIMIT),
        name="finish_keys_values",
    )(flags, table, cosine, sine, *kept, side_back, cross_back)


def exchange(array, axes):
    return lax.all_to_all(array, axes, 0, 0)


def to_all(array, axes):
    count = lax.axis_size(axes)
    return exchange(jnp.broadcast_to(array[None], (count,) + array.shape), axes)


def add_up(array):
    return jnp.sum(array.astype(jnp.float32), axis=0).astype(jnp.bfloat16)


def local(query, keys, values, out_grad, query_lowrank_state, value_lowrank_state, shift_flags):
    ctx_index = lax.axis_index(SEQ_AXES)
    ctx_count = lax.axis_size(SEQ_AXES)

    def send(array, to):
        pairs = [(i, to(i) % ctx_count) for i in range(ctx_count) if to(i) is not None]
        return lax.ppermute(array, SEQ_AXES, pairs)

    def flip(mask):
        return lambda i: i ^ mask

    def to_odd(i):
        return i + 2 if i // 2 % 2 == 0 else None

    def to_even(i):
        return i - 2 if i // 2 % 2 == 1 else None

    chip = ctx_index // 2
    light_half = chip // 2 % 2
    table = jnp.stack([chip % 2, ctx_index % 2, light_half, 1 - light_half]).astype(jnp.int32)

    both, light = pack(shift_flags, table, keys[0], values[0], value_lowrank_state[0].T)
    crossed = send(light, lambda i: i + GROUP_DEV // 2)
    sided = send(both, to_odd)
    both_other = send(both, flip(1))
    sided_other = send(sided, flip(1))
    half_dim = HEAD_WIDTH // 2
    positions = ctx_index * TOK_DEV + jnp.arange(TOK_DEV, dtype=jnp.int32)
    inv_freq = 10000.0 ** (-(jnp.arange(half_dim, dtype=jnp.float32) * 2.0) / HEAD_WIDTH)
    angles = positions.astype(jnp.float32)[:, None] * inv_freq[None, :]
    cos_half, sin_half = jnp.cos(angles), jnp.sin(angles)
    cosine = jnp.concatenate([cos_half, cos_half], axis=1)
    sine = jnp.concatenate([sin_half, -sin_half], axis=1)
    low = query_lowrank_state[0].T
    crossed, sided_other, both_other, cosine, sine, low = lax.optimization_barrier(
        (crossed, sided_other, both_other, cosine, sine, low)
    )
    crossed_other, swapped, swapped_other = (send(crossed, flip(mask)) for mask in (1, 2, 3))
    gq, terms, light_keep, light_send = attention(
        False, shift_flags, table, query[0], out_grad[0], [both, sided], [both_other, sided_other],
        cosine, sine, low, None,
    )
    gq, terms, heavy_keep, heavy_send, swap_keep, swap_send = attention(
        True, shift_flags, table, query[0], out_grad[0],
        [both, crossed[None], swapped[None], sided],
        [both_other, crossed_other[None], swapped_other[None], sided_other],
        cosine, sine, low, (gq, terms),
    )

    light_from = send(light_send, flip(1))
    heavy_from = send(heavy_send, flip(1))
    swap_from = send(swap_keep, flip(2))
    swap_far = send(swap_send, flip(3))
    terms = exchange(terms, "zc")
    terms, light_from, heavy_from, swap_from, swap_far = lax.optimization_barrier(
        (terms, light_from, heavy_from, swap_from, swap_far)
    )

    def wide(array):
        return array.astype(jnp.float32)

    cross_part = heavy_keep[1] + wide(heavy_from[1]) + wide(swap_from) + wide(swap_far)
    side_part = jnp.stack([light_keep[1] + wide(light_from[1]), heavy_keep[2] + wide(heavy_from[2])])
    cross_back = send(cross_part.astype(jnp.bfloat16), lambda i: i - GROUP_DEV // 2)
    side_back = send(side_part.astype(jnp.bfloat16), to_even)
    terms = to_all(add_up(terms), SUM_AXES)
    terms, cross_back, side_back = lax.optimization_barrier((terms, cross_back, side_back))
    gk, gv = finish(
        shift_flags, table, cosine, sine, [light_keep, light_from, heavy_keep, heavy_from],
        side_back, cross_back,
    )
    terms = to_all(add_up(terms), "zc")
    query_terms = terms[:, : 2 * RANK].reshape(QUERY_HEADS_HALF, RANK, HEAD_WIDTH)
    pair_rows = 2 * RANK // PER_GROUP
    value_terms = terms[:, 2 * RANK : 2 * RANK + pair_rows].reshape(
        KEY_VALUE_HEADS, RANK, HEAD_WIDTH
    )

    def rank_rows(heads):
        return wide(jnp.transpose(heads, (1, 0, 2)).reshape(RANK, -1))

    return gq[None], gk[None], gv[None], rank_rows(query_terms), rank_rows(value_terms)


def solution(mesh):
    dp, ctx = mesh.shape["dp"], mesh.shape["ctx"]
    split = Mesh(mesh.devices.reshape(dp, ctx // PEERS, PEERS), ("dp", "yh", "zc"))
    rows = P("dp", SEQ_AXES, None)
    return jax.shard_map(
        local,
        mesh=split,
        in_specs=(rows,) * 6 + (P(),),
        out_specs=(rows, rows, rows, P(), P()),
        check_vma=False,
    )
```

```python
from functools import partial
import math

import jax
import jax.numpy as jnp
from jax import lax
from jax.experimental import pallas as pl
from jax.experimental.pallas import tpu as pltpu
from jax.sharding import Mesh, PartitionSpec as P

QUERY_HEADS_HALF = 32
KEY_VALUE_HEADS = 4
HEAD_WIDTH = 128
GROUP_DEV = 8
TOK_DEV = 128
HALF_KV = KEY_VALUE_HEADS // 2
PER_GROUP = QUERY_HEADS_HALF // KEY_VALUE_HEADS
RANK = 8
PACK_ROWS = 4 * TOK_DEV + 16
TERM_ROWS = 16
ADAPTER_SCALE = 2.0
SCORE_SCALE = 1.0 / math.sqrt(HEAD_WIDTH)
EXP2_SCALE = SCORE_SCALE * math.log2(math.e)
MASKED = -1e30
NT = (((1,), (1,)), ((), ()))
TN = (((0,), (0,)), ((), ()))
VMEM_LIMIT = 20 * 1024 * 1024
SEQ_AXES = ("yh", "zc")
SUM_AXES = ("dp", "yh")


def head_of(flags, half, sub):
    hit = [flags[head] == half for head in range(KEY_VALUE_HEADS)]
    low = jnp.where(hit[0], 0, jnp.where(hit[1], 1, 2))
    high = jnp.where(hit[3], 3, jnp.where(hit[2], 2, 1))
    return jnp.where(sub == 0, low, high)


def columns_of(head):
    return pl.ds(pl.multiple_of(head * HEAD_WIDTH, HEAD_WIDTH), HEAD_WIDTH)


def pack_kernel(flags_ref, table_ref, keys_ref, values_ref, low_ref, both_ref, light_ref):
    low = low_ref[...].astype(jnp.float32)
    low = jnp.concatenate([low, jnp.zeros_like(low)], axis=0).astype(jnp.bfloat16)
    for place in range(2):
        half = table_ref[2 + place]
        for sub in range(HALF_KV):
            columns = columns_of(head_of(flags_ref, half, sub))
            for kind, ref in enumerate((keys_ref, values_ref)):
                rows = slice((2 * kind + sub) * TOK_DEV, (2 * kind + sub + 1) * TOK_DEV)
                both_ref[place, rows, :] = ref[:, columns]
                if place == 0:
                    light_ref[rows, :] = ref[:, columns]
        both_ref[place, 4 * TOK_DEV :, :] = low
    light_ref[4 * TOK_DEV :, :] = low


def pack(flags, table, keys, values, low):
    whole = pl.BlockSpec(memory_space=pltpu.VMEM)
    scalars = pl.BlockSpec(memory_space=pltpu.SMEM)
    return pl.pallas_call(
        pack_kernel,
        out_shape=(
            jax.ShapeDtypeStruct((2, PACK_ROWS, HEAD_WIDTH), jnp.bfloat16),
            jax.ShapeDtypeStruct((PACK_ROWS, HEAD_WIDTH), jnp.bfloat16),
        ),
        in_specs=[scalars, scalars, whole, whole, whole],
        out_specs=(whole, whole),
        name="pack_heads",
    )(flags, table, keys, values, low)


def attention_kernel(heavy, flags_ref, table_ref, q_ref, d_ref, *refs):
    chunks = 4 if heavy else 2
    mine, other = refs[:chunks], refs[chunks : 2 * chunks]
    cos_ref, sin_ref, low_ref = refs[2 * chunks : 2 * chunks + 3]
    gq_ref, term_ref, keep_ref, send_ref = refs[len(refs) - 9 : len(refs) - 5]
    k_all, v_all, low_all, dk_ref, dv_ref = refs[len(refs) - 5 :]
    sub = pl.program_id(0)
    odd, core = table_ref[0], table_ref[1]
    rows = 2 * TOK_DEV
    wide = PER_GROUP * TOK_DEV
    k_rows = pl.ds(pl.multiple_of(sub * TOK_DEV, TOK_DEV), TOK_DEV)
    v_rows = pl.ds(pl.multiple_of((2 + sub) * TOK_DEV, TOK_DEV), TOK_DEV)

    def branch(n):
        for j in range(n):
            for c, side in enumerate((mine[j], other[j])):
                span = slice(j * rows + c * TOK_DEV, j * rows + (c + 1) * TOK_DEV)
                k_all[span, :] = side[0, k_rows, :]
                v_all[span, :] = side[0, v_rows, :]
                low_all[:, span] = side[0, 4 * TOK_DEV :, :]
        width = n * rows
        key = lax.broadcasted_iota(jnp.int32, (rows, wide), 0)
        row = lax.broadcasted_iota(jnp.int32, (rows, wide), 1) % TOK_DEV
        limit = jnp.where(core == 1, rows, 0)
        allowed = (key <= row) | ((key >= TOK_DEV) & (key < limit))

        def stacked(ref):
            return jnp.concatenate(
                [ref[:, h * HEAD_WIDTH : (h + 1) * HEAD_WIDTH] for h in range(PER_GROUP)], axis=0
            )

        q = stacked(q_ref)
        d = stacked(d_ref)
        k = k_all[:width, :]
        s = lax.dot_general(k, q, NT, preferred_element_type=jnp.float32)
        near = jnp.where(allowed, s[:rows], MASKED)
        s = near if n == 1 else jnp.concatenate([near, s[rows:]], axis=0)
        dp = lax.dot_general(v_all[:width, :], d, NT, preferred_element_type=jnp.float32)
        top = jnp.max(s, axis=0, keepdims=True) * EXP2_SCALE
        p = jnp.exp2(s * EXP2_SCALE - top)
        inverse = 1.0 / jnp.sum(p, axis=0, keepdims=True)
        delta = jnp.sum(p * dp, axis=0, keepdims=True) * inverse
        p = p * inverse
        ds = (p * (dp - delta)).astype(jnp.bfloat16)
        dv_ref[:width, :] = jnp.dot(p.astype(jnp.bfloat16), d, preferred_element_type=jnp.float32)
        dk_ref[:width, :] = jnp.dot(ds, q, preferred_element_type=jnp.float32)
        dq = lax.dot_general(ds, k, TN, preferred_element_type=jnp.float32) * SCORE_SCALE
        low_rank = low_ref[...]
        parts = []
        for h in range(PER_GROUP):
            x = dq[h * TOK_DEV : (h + 1) * TOK_DEV, :]
            turned = x * cos_ref[...] + pltpu.roll(x, HEAD_WIDTH // 2, 1) * sin_ref[...]
            low = turned.astype(jnp.bfloat16)
            gq_ref[:, h * HEAD_WIDTH : (h + 1) * HEAD_WIDTH] = low
            parts.append(
                jnp.dot(low_rank, low, preferred_element_type=jnp.float32) * ADAPTER_SCALE
            )
        value_part = (
            jnp.dot(
                low_all[:, :width],
                dv_ref[:width, :].astype(jnp.bfloat16),
                preferred_element_type=jnp.float32,
            )
            * ADAPTER_SCALE
        )
        blank = jnp.zeros((TERM_ROWS - RANK - 1, HEAD_WIDTH), jnp.float32)
        for h in range(PER_GROUP):
            block = jnp.concatenate([parts[h], value_part[h : h + 1], blank], axis=0)
            term_ref[h] = block.astype(jnp.bfloat16)

        def store(ref, j, span):
            for grad_ref, to_rows in ((dk_ref, k_rows), (dv_ref, v_rows)):
                if j < n:
                    grad = grad_ref[j * rows + span * TOK_DEV : j * rows + (span + 1) * TOK_DEV, :]
                else:
                    grad = jnp.zeros((TOK_DEV, HEAD_WIDTH), jnp.float32)
                ref[to_rows, :] = grad.astype(ref.dtype)

        for j in range(chunks):
            store(keep_ref.at[j], j, 0)
            store(send_ref.at[j], j, 1)

    base = 3 if heavy else 1
    for more in range(2):
        pl.when(odd == more)(lambda n=base + more: branch(n))


def attention(heavy, flags, table, query, out_grad, mine, other, cosine, sine, low, before):
    tok = TOK_DEV
    wide = PER_GROUP * HEAD_WIDTH
    chunks = len(mine)
    keys = chunks * 2 * tok
    place = 1 if heavy else 0

    def whole(shape):
        return pl.BlockSpec(shape, lambda s, f, t: (0,) * len(shape))

    def head(f, t, s):
        return head_of(f, t[2 + place], s)

    columns = pl.BlockSpec((tok, wide), lambda s, f, t: (0, head(f, t, s)))
    terms = pl.BlockSpec((PER_GROUP, TERM_ROWS, HEAD_WIDTH), lambda s, f, t: (head(f, t, s), 0, 0))
    table_spec = whole((tok, HEAD_WIDTH))
    in_specs = [columns, columns]
    for array, at in (*mine, *other):
        in_specs.append(
            pl.BlockSpec((1, PACK_ROWS, HEAD_WIDTH), lambda s, f, t, at=at: (at, 0, 0))
        )
    in_specs += [table_spec, table_spec, whole((RANK, tok))]
    operands = [query, out_grad, *(array for array, at in (*mine, *other)), cosine, sine, low]
    aliases = {}
    if before is not None:
        for out, array in enumerate(before):
            aliases[2 + len(operands)] = out
            operands.append(array)
            in_specs.append(pl.BlockSpec(memory_space=pl.ANY))
    out_shape = [
        jax.ShapeDtypeStruct((tok, QUERY_HEADS_HALF * HEAD_WIDTH), jnp.bfloat16),
        jax.ShapeDtypeStruct((QUERY_HEADS_HALF, TERM_ROWS, HEAD_WIDTH), jnp.bfloat16),
        jax.ShapeDtypeStruct((chunks, 4 * tok, HEAD_WIDTH), jnp.float32),
        jax.ShapeDtypeStruct((chunks, 4 * tok, HEAD_WIDTH), jnp.bfloat16),
    ]
    return pl.pallas_call(
        partial(attention_kernel, heavy),
        grid_spec=pltpu.PrefetchScalarGridSpec(
            num_scalar_prefetch=2,
            grid=(HALF_KV,),
            in_specs=in_specs,
            out_specs=[columns, terms] + [whole(o.shape) for o in out_shape[2:]],
            scratch_shapes=[
                pltpu.VMEM((keys, HEAD_WIDTH), jnp.bfloat16),
                pltpu.VMEM((keys, HEAD_WIDTH), jnp.bfloat16),
                pltpu.VMEM((16, keys), jnp.bfloat16),
                pltpu.VMEM((keys, HEAD_WIDTH), jnp.float32),
                pltpu.VMEM((keys, HEAD_WIDTH), jnp.float32),
            ],
        ),
        out_shape=out_shape,
        input_output_aliases=aliases,
        compiler_params=pltpu.CompilerParams(
            dimension_semantics=("arbitrary",), vmem_limit_bytes=VMEM_LIMIT
        ),
        cost_estimate=pl.CostEstimate(
            flops=10 * HALF_KV * wide * keys * HEAD_WIDTH,
            bytes_accessed=6 << 20,
            transcendentals=HALF_KV * wide * keys,
        ),
        name="attention_heavy" if heavy else "attention_light",
    )(flags, table, *operands)


def finish_kernel(flags_ref, table_ref, cos_ref, sin_ref, *refs):
    light_keep, heavy_keep, light_from, heavy_from, side_ref, cross_ref, gk_ref, gv_ref = refs
    for place, (keep_ref, from_ref) in enumerate(
        ((light_keep, light_from), (heavy_keep, heavy_from))
    ):
        total = keep_ref[0] + from_ref[0].astype(jnp.float32) + side_ref[place].astype(jnp.float32)
        if place == 0:
            total += cross_ref[...].astype(jnp.float32)
        for sub in range(HALF_KV):
            columns = columns_of(head_of(flags_ref, table_ref[2 + place], sub))
            dk = total[sub * TOK_DEV : (sub + 1) * TOK_DEV] * SCORE_SCALE
            turned = dk * cos_ref[...] + pltpu.roll(dk, HEAD_WIDTH // 2, 1) * sin_ref[...]
            gk_ref[:, columns] = turned.astype(jnp.bfloat16)
            dv = total[(2 + sub) * TOK_DEV : (3 + sub) * TOK_DEV]
            gv_ref[:, columns] = dv.astype(jnp.bfloat16)


def finish(flags, table, cosine, sine, light_keep, heavy_keep, pair_from, side_back, cross_back):
    tok = TOK_DEV

    def whole(shape):
        return pl.BlockSpec(shape, lambda i, f, t: (0,) * len(shape))

    def block(at):
        return pl.BlockSpec((1, 4 * tok, HEAD_WIDTH), lambda i, f, t: (at, 0, 0))

    shape = jax.ShapeDtypeStruct((tok, KEY_VALUE_HEADS * HEAD_WIDTH), jnp.bfloat16)
    return pl.pallas_call(
        finish_kernel,
        grid_spec=pltpu.PrefetchScalarGridSpec(
            num_scalar_prefetch=2,
            grid=(1,),
            in_specs=[whole((tok, HEAD_WIDTH))] * 2
            + [block(0), block(0), block(0), block(2)]
            + [whole(side_back.shape), whole(cross_back.shape)],
            out_specs=[whole(shape.shape)] * 2,
        ),
        out_shape=[shape, shape],
        compiler_params=pltpu.CompilerParams(vmem_limit_bytes=VMEM_LIMIT),
        name="finish_keys_values",
    )(flags, table, cosine, sine, light_keep, heavy_keep, pair_from, pair_from, side_back, cross_back)


def exchange(array, axes):
    return lax.all_to_all(array, axes, 0, 0)


def to_all(array, axes):
    count = lax.axis_size(axes)
    return exchange(jnp.broadcast_to(array[None], (count,) + array.shape), axes)


def add_up(array):
    return jnp.sum(array.astype(jnp.float32), axis=0).astype(jnp.bfloat16)


def local(query, keys, values, out_grad, query_lowrank_state, value_lowrank_state, shift_flags):
    ctx_index = lax.axis_index(SEQ_AXES)
    ctx_count = lax.axis_size(SEQ_AXES)

    def send(array, to):
        pairs = [(i, to(i) % ctx_count) for i in range(ctx_count) if to(i) is not None]
        return lax.ppermute(array, SEQ_AXES, pairs)

    def flip(mask):
        return lambda i: i ^ mask

    def to_odd(i):
        return i + 2 if i // 2 % 2 == 0 else None

    def to_even(i):
        return i - 2 if i // 2 % 2 == 1 else None

    chip = ctx_index // 2
    light_half = chip // 2 % 2
    table = jnp.stack([chip % 2, ctx_index % 2, light_half, 1 - light_half]).astype(jnp.int32)

    both, light = pack(shift_flags, table, keys[0], values[0], value_lowrank_state[0].T)
    crossed = send(light, lambda i: i + GROUP_DEV // 2)
    sided = send(both, to_odd)
    half_dim = HEAD_WIDTH // 2
    positions = ctx_index * TOK_DEV + jnp.arange(TOK_DEV, dtype=jnp.int32)
    inv_freq = 10000.0 ** (-(jnp.arange(half_dim, dtype=jnp.float32) * 2.0) / HEAD_WIDTH)
    angles = positions.astype(jnp.float32)[:, None] * inv_freq[None, :]
    cos_half, sin_half = jnp.cos(angles), jnp.sin(angles)
    cosine = jnp.concatenate([cos_half, cos_half], axis=1)
    sine = jnp.concatenate([sin_half, -sin_half], axis=1)
    low = query_lowrank_state[0].T
    crossed, sided, cosine, sine, low = lax.optimization_barrier(
        (crossed, sided, cosine, sine, low)
    )
    crossed = crossed[None]
    swapped = send(crossed, flip(2))
    arrived = send(jnp.concatenate([both, sided, crossed]), flip(1))
    swapped_other = send(crossed, flip(3))
    gq, terms, light_keep, light_send = attention(
        False, shift_flags, table, query[0], out_grad[0],
        [(both, 0), (sided, 0)], [(arrived, 0), (arrived, 2)],
        cosine, sine, low, None,
    )
    gq, terms, heavy_keep, heavy_send = attention(
        True, shift_flags, table, query[0], out_grad[0],
        [(both, 1), (crossed, 0), (swapped, 0), (sided, 1)],
        [(arrived, 1), (arrived, 4), (swapped_other, 0), (arrived, 3)],
        cosine, sine, low, (gq, terms),
    )

    def wide(array):
        return array.astype(jnp.float32)

    def sent(array):
        return array.astype(jnp.bfloat16)

    terms = exchange(terms, SUM_AXES)
    pair_from = send(jnp.concatenate([light_send, heavy_send]), flip(1))
    swap_from = send(sent(heavy_keep[2] + wide(pair_from[4])), flip(2))
    terms, pair_from, swap_from = lax.optimization_barrier((terms, pair_from, swap_from))
    cross_back = send(
        sent(heavy_keep[1] + wide(pair_from[3]) + wide(swap_from)), lambda i: i - GROUP_DEV // 2
    )
    side_back = send(
        sent(jnp.stack([light_keep[1] + wide(pair_from[1]), heavy_keep[3] + wide(pair_from[5])])),
        to_even,
    )
    terms = to_all(add_up(terms)[: RANK + 1], "zc")
    gk, gv = finish(
        shift_flags, table, cosine, sine, light_keep, heavy_keep, pair_from, side_back, cross_back
    )
    terms = to_all(add_up(terms), SUM_AXES)
    query_terms = terms[:, :RANK]
    value_terms = terms[:, RANK].reshape(KEY_VALUE_HEADS, RANK, HEAD_WIDTH)

    def rank_rows(heads):
        return wide(jnp.transpose(heads, (1, 0, 2)).reshape(RANK, -1))

    return gq[None], gk[None], gv[None], rank_rows(query_terms), rank_rows(value_terms)


def solution(mesh):
    dp, ctx = mesh.shape["dp"], mesh.shape["ctx"]
    split = Mesh(mesh.devices.reshape(dp, 2, ctx // 2), ("dp", "yh", "zc"))
    rows = P("dp", SEQ_AXES, None)
    return jax.shard_map(
        local,
        mesh=split,
        in_specs=(rows,) * 6 + (P(),),
        out_specs=(rows, rows, rows, P(), P()),
        check_vma=False,
    )
```

```python
from functools import partial
import math

import jax
import jax.numpy as jnp
from jax import lax
from jax.experimental import pallas as pl
from jax.experimental.pallas import tpu as pltpu
from jax.sharding import Mesh, PartitionSpec as P

QUERY_HEADS_HALF = 32
KEY_VALUE_HEADS = 4
HEAD_WIDTH = 128
GROUP_DEV = 8
TOK_DEV = 128
HALF_KV = KEY_VALUE_HEADS // 2
PER_GROUP = QUERY_HEADS_HALF // KEY_VALUE_HEADS
RANK = 8
PACK_ROWS = 4 * TOK_DEV + 16
TERM_ROWS = 16
ADAPTER_SCALE = 2.0
SCORE_SCALE = 1.0 / math.sqrt(HEAD_WIDTH)
EXP2_SCALE = SCORE_SCALE * math.log2(math.e)
MASKED = -1e30
NT = (((1,), (1,)), ((), ()))
TN = (((0,), (0,)), ((), ()))
VMEM_LIMIT = 20 * 1024 * 1024
SEQ_AXES = ("yh", "zc")
SUM_AXES = ("dp", "yh")


def head_of(flags, half, sub):
    hit = [flags[head] == half for head in range(KEY_VALUE_HEADS)]
    low = jnp.where(hit[0], 0, jnp.where(hit[1], 1, 2))
    high = jnp.where(hit[3], 3, jnp.where(hit[2], 2, 1))
    return jnp.where(sub == 0, low, high)


def columns_of(head):
    return pl.ds(pl.multiple_of(head * HEAD_WIDTH, HEAD_WIDTH), HEAD_WIDTH)


def pack_kernel(flags_ref, table_ref, keys_ref, values_ref, low_ref, both_ref, light_ref):
    low = low_ref[...].astype(jnp.float32)
    low = jnp.concatenate([low, jnp.zeros_like(low)], axis=0).astype(jnp.bfloat16)
    for place in range(2):
        half = table_ref[2 + place]
        for sub in range(HALF_KV):
            columns = columns_of(head_of(flags_ref, half, sub))
            for kind, ref in enumerate((keys_ref, values_ref)):
                rows = slice((2 * kind + sub) * TOK_DEV, (2 * kind + sub + 1) * TOK_DEV)
                both_ref[place, rows, :] = ref[:, columns]
                if place == 0:
                    light_ref[rows, :] = ref[:, columns]
        both_ref[place, 4 * TOK_DEV :, :] = low
    light_ref[4 * TOK_DEV :, :] = low


def pack(flags, table, keys, values, low):
    whole = pl.BlockSpec(memory_space=pltpu.VMEM)
    scalars = pl.BlockSpec(memory_space=pltpu.SMEM)
    return pl.pallas_call(
        pack_kernel,
        out_shape=(
            jax.ShapeDtypeStruct((2, PACK_ROWS, HEAD_WIDTH), jnp.bfloat16),
            jax.ShapeDtypeStruct((PACK_ROWS, HEAD_WIDTH), jnp.bfloat16),
        ),
        in_specs=[scalars, scalars, whole, whole, whole],
        out_specs=(whole, whole),
        name="pack_heads",
    )(flags, table, keys, values, low)


def stage_kernel(flags_ref, table_ref, query_ref, out_grad_ref, *outs):
    for place in range(2):
        for sub in range(HALF_KV):
            head = head_of(flags_ref, table_ref[2 + place], sub)
            for h in range(PER_GROUP):
                start = (sub * PER_GROUP + h) * TOK_DEV
                for kind, ref in enumerate((query_ref, out_grad_ref)):
                    outs[2 * place + kind][start : start + TOK_DEV, :] = ref[
                        :, columns_of(head * PER_GROUP + h)
                    ]


def stage(flags, table, query, out_grad):
    whole = pl.BlockSpec(memory_space=pltpu.VMEM)
    scalars = pl.BlockSpec(memory_space=pltpu.SMEM)
    shape = jax.ShapeDtypeStruct((HALF_KV * PER_GROUP * TOK_DEV, HEAD_WIDTH), jnp.bfloat16)
    outs = pl.pallas_call(
        stage_kernel,
        out_shape=[shape] * 4,
        in_specs=[scalars, scalars, whole, whole],
        out_specs=[whole] * 4,
        compiler_params=pltpu.CompilerParams(vmem_limit_bytes=VMEM_LIMIT),
        name="stage_rows",
    )(flags, table, query, out_grad)
    return outs[:2], outs[2:]


def attention_kernel(heavy, flags_ref, table_ref, q_ref, d_ref, *refs):
    chunks = 4 if heavy else 2
    mine, other = refs[:chunks], refs[chunks : 2 * chunks]
    cos_ref, sin_ref, low_ref = refs[2 * chunks : 2 * chunks + 3]
    before_ref = refs[2 * chunks + 3] if heavy else None
    gq_ref, term_ref, keep_ref, send_ref = refs[len(refs) - 9 : len(refs) - 5]
    k_all, v_all, low_all, dk_ref, dv_ref = refs[len(refs) - 5 :]
    sub = pl.program_id(0)
    odd, core = table_ref[0], table_ref[1]
    rows = 2 * TOK_DEV
    wide = PER_GROUP * TOK_DEV
    k_rows = pl.ds(pl.multiple_of(sub * TOK_DEV, TOK_DEV), TOK_DEV)
    v_rows = pl.ds(pl.multiple_of((2 + sub) * TOK_DEV, TOK_DEV), TOK_DEV)

    def branch(n):
        for j in range(n):
            for c, side in enumerate((mine[j], other[j])):
                span = slice(j * rows + c * TOK_DEV, j * rows + (c + 1) * TOK_DEV)
                k_all[span, :] = side[0, k_rows, :]
                v_all[span, :] = side[0, v_rows, :]
                low_all[:, span] = side[0, 4 * TOK_DEV :, :]
        width = n * rows
        key = lax.broadcasted_iota(jnp.int32, (rows, wide), 0)
        row = lax.broadcasted_iota(jnp.int32, (rows, wide), 1) % TOK_DEV
        limit = jnp.where(core == 1, rows, 0)
        allowed = (key <= row) | ((key >= TOK_DEV) & (key < limit))

        q = q_ref[...]
        d = d_ref[...]
        k = k_all[:width, :]
        s = lax.dot_general(k, q, NT, preferred_element_type=jnp.float32)
        near = jnp.where(allowed, s[:rows], MASKED)
        s = near if n == 1 else jnp.concatenate([near, s[rows:]], axis=0)
        dp = lax.dot_general(v_all[:width, :], d, NT, preferred_element_type=jnp.float32)
        top = jnp.max(s, axis=0, keepdims=True) * EXP2_SCALE
        p = jnp.exp2(s * EXP2_SCALE - top)
        inverse = 1.0 / jnp.sum(p, axis=0, keepdims=True)
        delta = jnp.sum(p * dp, axis=0, keepdims=True) * inverse
        p = p * inverse
        ds = (p * (dp - delta)).astype(jnp.bfloat16)
        dv_ref[:width, :] = jnp.dot(p.astype(jnp.bfloat16), d, preferred_element_type=jnp.float32)
        dk_ref[:width, :] = jnp.dot(ds, q, preferred_element_type=jnp.float32)
        dq = lax.dot_general(ds, k, TN, preferred_element_type=jnp.float32) * SCORE_SCALE
        low_rank = low_ref[...]
        parts = []
        for h in range(PER_GROUP):
            x = dq[h * TOK_DEV : (h + 1) * TOK_DEV, :]
            turned = x * cos_ref[...] + pltpu.roll(x, HEAD_WIDTH // 2, 1) * sin_ref[...]
            low = turned.astype(jnp.bfloat16)
            gq_ref[:, h * HEAD_WIDTH : (h + 1) * HEAD_WIDTH] = low
            parts.append(
                jnp.dot(low_rank, low, preferred_element_type=jnp.float32) * ADAPTER_SCALE
            )
        value_part = (
            jnp.dot(
                low_all[:, :width],
                dv_ref[:width, :].astype(jnp.bfloat16),
                preferred_element_type=jnp.float32,
            )
            * ADAPTER_SCALE
        )
        blank = jnp.zeros((TERM_ROWS - RANK - 1, HEAD_WIDTH), jnp.float32)
        for h in range(PER_GROUP):
            block = jnp.concatenate([parts[h], value_part[h : h + 1], blank], axis=0)
            term_ref[h] = block.astype(jnp.bfloat16)

        def store(ref, j, span):
            for grad_ref, to_rows in ((dk_ref, k_rows), (dv_ref, v_rows)):
                if j < n:
                    grad = grad_ref[j * rows + span * TOK_DEV : j * rows + (span + 1) * TOK_DEV, :]
                else:
                    grad = jnp.zeros((TOK_DEV, HEAD_WIDTH), jnp.float32)
                ref[to_rows, :] = grad.astype(ref.dtype)

        first = 2 if heavy else 0
        for j in range(chunks):
            store(keep_ref.at[j], j, 0)
            store(send_ref.at[first + j], j, 1)

    if heavy:

        @pl.when(sub == 0)
        def _():
            send_ref[:2] = before_ref[...]

    base = 3 if heavy else 1
    for more in range(2):
        pl.when(odd == more)(lambda n=base + more: branch(n))


def attention(heavy, flags, table, rows, mine, other, cosine, sine, low, before):
    tok = TOK_DEV
    wide = PER_GROUP * HEAD_WIDTH
    chunks = len(mine)
    keys = chunks * 2 * tok
    place = 1 if heavy else 0

    def whole(shape):
        return pl.BlockSpec(shape, lambda s, f, t: (0,) * len(shape))

    def head(f, t, s):
        return head_of(f, t[2 + place], s)

    columns = pl.BlockSpec((tok, wide), lambda s, f, t: (0, head(f, t, s)))
    terms = pl.BlockSpec((PER_GROUP, TERM_ROWS, HEAD_WIDTH), lambda s, f, t: (head(f, t, s), 0, 0))
    table_spec = whole((tok, HEAD_WIDTH))
    stacked = pl.BlockSpec((wide, HEAD_WIDTH), lambda s, f, t: (s, 0))
    in_specs = [stacked, stacked]
    for array, at in (*mine, *other):
        in_specs.append(
            pl.BlockSpec((1, PACK_ROWS, HEAD_WIDTH), lambda s, f, t, at=at: (at, 0, 0))
        )
    in_specs += [table_spec, table_spec, whole((RANK, tok))]
    operands = [*rows, *(array for array, at in (*mine, *other)), cosine, sine, low]
    aliases = {}
    if heavy:
        *before, light_send = before
        operands.append(light_send)
        in_specs.append(whole(light_send.shape))
        for out, array in enumerate(before):
            aliases[2 + len(operands)] = out
            operands.append(array)
            in_specs.append(pl.BlockSpec(memory_space=pl.ANY))
    out_shape = [
        jax.ShapeDtypeStruct((tok, QUERY_HEADS_HALF * HEAD_WIDTH), jnp.bfloat16),
        jax.ShapeDtypeStruct((QUERY_HEADS_HALF, TERM_ROWS, HEAD_WIDTH), jnp.bfloat16),
        jax.ShapeDtypeStruct((chunks, 4 * tok, HEAD_WIDTH), jnp.float32),
        jax.ShapeDtypeStruct((6 if heavy else 2, 4 * tok, HEAD_WIDTH), jnp.bfloat16),
    ]
    return pl.pallas_call(
        partial(attention_kernel, heavy),
        grid_spec=pltpu.PrefetchScalarGridSpec(
            num_scalar_prefetch=2,
            grid=(HALF_KV,),
            in_specs=in_specs,
            out_specs=[columns, terms] + [whole(o.shape) for o in out_shape[2:]],
            scratch_shapes=[
                pltpu.VMEM((keys, HEAD_WIDTH), jnp.bfloat16),
                pltpu.VMEM((keys, HEAD_WIDTH), jnp.bfloat16),
                pltpu.VMEM((16, keys), jnp.bfloat16),
                pltpu.VMEM((keys, HEAD_WIDTH), jnp.float32),
                pltpu.VMEM((keys, HEAD_WIDTH), jnp.float32),
            ],
        ),
        out_shape=out_shape,
        input_output_aliases=aliases,
        compiler_params=pltpu.CompilerParams(
            dimension_semantics=("arbitrary",), vmem_limit_bytes=VMEM_LIMIT
        ),
        cost_estimate=pl.CostEstimate(
            flops=10 * HALF_KV * wide * keys * HEAD_WIDTH,
            bytes_accessed=6 << 20,
            transcendentals=HALF_KV * wide * keys,
        ),
        name="attention_heavy" if heavy else "attention_light",
    )(flags, table, *operands)


def finish_kernel(flags_ref, table_ref, cos_ref, sin_ref, *refs):
    light_keep, heavy_keep, light_from, heavy_from, side_ref, cross_ref, gk_ref, gv_ref = refs
    for place, (keep_ref, from_ref) in enumerate(
        ((light_keep, light_from), (heavy_keep, heavy_from))
    ):
        total = keep_ref[0] + from_ref[0].astype(jnp.float32) + side_ref[place].astype(jnp.float32)
        if place == 0:
            total += cross_ref[...].astype(jnp.float32)
        for sub in range(HALF_KV):
            columns = columns_of(head_of(flags_ref, table_ref[2 + place], sub))
            dk = total[sub * TOK_DEV : (sub + 1) * TOK_DEV] * SCORE_SCALE
            turned = dk * cos_ref[...] + pltpu.roll(dk, HEAD_WIDTH // 2, 1) * sin_ref[...]
            gk_ref[:, columns] = turned.astype(jnp.bfloat16)
            dv = total[(2 + sub) * TOK_DEV : (3 + sub) * TOK_DEV]
            gv_ref[:, columns] = dv.astype(jnp.bfloat16)


def finish(flags, table, cosine, sine, light_keep, heavy_keep, pair_from, side_back, cross_back):
    tok = TOK_DEV

    def whole(shape):
        return pl.BlockSpec(shape, lambda i, f, t: (0,) * len(shape))

    def block(at):
        return pl.BlockSpec((1, 4 * tok, HEAD_WIDTH), lambda i, f, t: (at, 0, 0))

    shape = jax.ShapeDtypeStruct((tok, KEY_VALUE_HEADS * HEAD_WIDTH), jnp.bfloat16)
    return pl.pallas_call(
        finish_kernel,
        grid_spec=pltpu.PrefetchScalarGridSpec(
            num_scalar_prefetch=2,
            grid=(1,),
            in_specs=[whole((tok, HEAD_WIDTH))] * 2
            + [block(0), block(0), block(0), block(2)]
            + [whole(side_back.shape), whole(cross_back.shape)],
            out_specs=[whole(shape.shape)] * 2,
        ),
        out_shape=[shape, shape],
        compiler_params=pltpu.CompilerParams(vmem_limit_bytes=VMEM_LIMIT),
        name="finish_keys_values",
    )(flags, table, cosine, sine, light_keep, heavy_keep, pair_from, pair_from, side_back, cross_back)


def exchange(array, axes):
    return lax.all_to_all(array, axes, 0, 0)


def to_all(array, axes):
    count = lax.axis_size(axes)
    return exchange(jnp.broadcast_to(array[None], (count,) + array.shape), axes)


def add_up(array):
    return jnp.sum(array.astype(jnp.float32), axis=0).astype(jnp.bfloat16)


def local(query, keys, values, out_grad, query_lowrank_state, value_lowrank_state, shift_flags):
    ctx_index = lax.axis_index(SEQ_AXES)
    ctx_count = lax.axis_size(SEQ_AXES)

    def send(array, to):
        pairs = [(i, to(i) % ctx_count) for i in range(ctx_count) if to(i) is not None]
        return lax.ppermute(array, SEQ_AXES, pairs)

    def flip(mask):
        return lambda i: i ^ mask

    def to_odd(i):
        return i + 2 if i // 2 % 2 == 0 else None

    def to_even(i):
        return i - 2 if i // 2 % 2 == 1 else None

    chip = ctx_index // 2
    light_half = chip // 2 % 2
    table = jnp.stack([chip % 2, ctx_index % 2, light_half, 1 - light_half]).astype(jnp.int32)

    both, light = pack(shift_flags, table, keys[0], values[0], value_lowrank_state[0].T)
    crossed = send(light, lambda i: i + GROUP_DEV // 2)
    sided = send(both, to_odd)
    half_dim = HEAD_WIDTH // 2
    positions = ctx_index * TOK_DEV + jnp.arange(TOK_DEV, dtype=jnp.int32)
    inv_freq = 10000.0 ** (-(jnp.arange(half_dim, dtype=jnp.float32) * 2.0) / HEAD_WIDTH)
    angles = positions.astype(jnp.float32)[:, None] * inv_freq[None, :]
    cos_half, sin_half = jnp.cos(angles), jnp.sin(angles)
    cosine = jnp.concatenate([cos_half, cos_half], axis=1)
    sine = jnp.concatenate([sin_half, -sin_half], axis=1)
    low = query_lowrank_state[0].T
    light_rows, heavy_rows = stage(shift_flags, table, query[0], out_grad[0])
    crossed, sided, cosine, sine, low, light_rows, heavy_rows = lax.optimization_barrier(
        (crossed, sided, cosine, sine, low, light_rows, heavy_rows)
    )
    crossed = crossed[None]
    swapped = send(crossed, flip(2))
    arrived = send(jnp.concatenate([both, sided, crossed]), flip(1))
    swapped_other = send(crossed, flip(3))
    gq, terms, light_keep, light_send = attention(
        False, shift_flags, table, light_rows,
        [(both, 0), (sided, 0)], [(arrived, 0), (arrived, 2)],
        cosine, sine, low, None,
    )
    gq, terms, heavy_keep, pair_send = attention(
        True, shift_flags, table, heavy_rows,
        [(both, 1), (crossed, 0), (swapped, 0), (sided, 1)],
        [(arrived, 1), (arrived, 4), (swapped_other, 0), (arrived, 3)],
        cosine, sine, low, (gq, terms, light_send),
    )

    def wide(array):
        return array.astype(jnp.float32)

    def sent(array):
        return array.astype(jnp.bfloat16)

    terms = exchange(terms, SUM_AXES)
    pair_from = send(pair_send, flip(1))
    swap_from = send(sent(heavy_keep[2] + wide(pair_from[4])), flip(2))
    terms, pair_from, swap_from = lax.optimization_barrier((terms, pair_from, swap_from))
    cross_back = send(
        sent(heavy_keep[1] + wide(pair_from[3]) + wide(swap_from)), lambda i: i - GROUP_DEV // 2
    )
    side_back = send(
        sent(jnp.stack([light_keep[1] + wide(pair_from[1]), heavy_keep[3] + wide(pair_from[5])])),
        to_even,
    )
    terms = to_all(add_up(terms)[: RANK + 1], "zc")
    gk, gv = finish(
        shift_flags, table, cosine, sine, light_keep, heavy_keep, pair_from, side_back, cross_back
    )
    terms = to_all(add_up(terms), SUM_AXES)
    query_terms = terms[:, :RANK]
    value_terms = terms[:, RANK].reshape(KEY_VALUE_HEADS, RANK, HEAD_WIDTH)

    def rank_rows(heads):
        return wide(jnp.transpose(heads, (1, 0, 2)).reshape(RANK, -1))

    return gq[None], gk[None], gv[None], rank_rows(query_terms), rank_rows(value_terms)


def solution(mesh):
    dp, ctx = mesh.shape["dp"], mesh.shape["ctx"]
    split = Mesh(mesh.devices.reshape(dp, 2, ctx // 2), ("dp", "yh", "zc"))
    rows = P("dp", SEQ_AXES, None)
    return jax.shard_map(
        local,
        mesh=split,
        in_specs=(rows,) * 6 + (P(),),
        out_specs=(rows, rows, rows, P(), P()),
        check_vma=False,
    )
```

```python
from functools import partial
import math

import jax
import jax.numpy as jnp
from jax import lax
from jax.experimental import pallas as pl
from jax.experimental.pallas import tpu as pltpu
from jax.sharding import Mesh, PartitionSpec as P

QUERY_HEADS_HALF = 32
KEY_VALUE_HEADS = 4
HEAD_WIDTH = 128
GROUP_DEV = 8
TOK_DEV = 128
HALF_KV = KEY_VALUE_HEADS // 2
PER_GROUP = QUERY_HEADS_HALF // KEY_VALUE_HEADS
RANK = 8
PACK_ROWS = 4 * TOK_DEV + 16
PEERS = 16
TERM_ROWS = 32
TERM_HEADS = QUERY_HEADS_HALF // PEERS
TERM_USED = TERM_HEADS * (RANK + 1)
ADAPTER_SCALE = 2.0
SCORE_SCALE = 1.0 / math.sqrt(HEAD_WIDTH)
EXP2_SCALE = SCORE_SCALE * math.log2(math.e)
MASKED = -1e30
NT = (((1,), (1,)), ((), ()))
TN = (((0,), (0,)), ((), ()))
VMEM_LIMIT = 20 * 1024 * 1024
SEQ_AXES = ("yh", "zc")
SUM_AXES = ("dp", "yh")


def head_of(flags, half, sub):
    hit = [flags[head] == half for head in range(KEY_VALUE_HEADS)]
    low = jnp.where(hit[0], 0, jnp.where(hit[1], 1, 2))
    high = jnp.where(hit[3], 3, jnp.where(hit[2], 2, 1))
    return jnp.where(sub == 0, low, high)


def columns_of(head):
    return pl.ds(pl.multiple_of(head * HEAD_WIDTH, HEAD_WIDTH), HEAD_WIDTH)


def pack_kernel(flags_ref, table_ref, keys_ref, values_ref, low_ref, both_ref, light_ref):
    low = low_ref[...].astype(jnp.float32)
    low = jnp.concatenate([low, jnp.zeros_like(low)], axis=0).astype(jnp.bfloat16)
    for place in range(2):
        half = table_ref[2 + place]
        for sub in range(HALF_KV):
            columns = columns_of(head_of(flags_ref, half, sub))
            for kind, ref in enumerate((keys_ref, values_ref)):
                rows = slice((2 * kind + sub) * TOK_DEV, (2 * kind + sub + 1) * TOK_DEV)
                both_ref[place, rows, :] = ref[:, columns]
                if place == 0:
                    light_ref[rows, :] = ref[:, columns]
        both_ref[place, 4 * TOK_DEV :, :] = low
    light_ref[4 * TOK_DEV :, :] = low


def pack(flags, table, keys, values, low):
    whole = pl.BlockSpec(memory_space=pltpu.VMEM)
    scalars = pl.BlockSpec(memory_space=pltpu.SMEM)
    return pl.pallas_call(
        pack_kernel,
        out_shape=(
            jax.ShapeDtypeStruct((2, PACK_ROWS, HEAD_WIDTH), jnp.bfloat16),
            jax.ShapeDtypeStruct((PACK_ROWS, HEAD_WIDTH), jnp.bfloat16),
        ),
        in_specs=[scalars, scalars, whole, whole, whole],
        out_specs=(whole, whole),
        name="pack_heads",
    )(flags, table, keys, values, low)


def stage_kernel(flags_ref, table_ref, query_ref, out_grad_ref, *outs):
    for place in range(2):
        for sub in range(HALF_KV):
            head = head_of(flags_ref, table_ref[2 + place], sub)
            for h in range(PER_GROUP):
                start = (sub * PER_GROUP + h) * TOK_DEV
                for kind, ref in enumerate((query_ref, out_grad_ref)):
                    outs[2 * place + kind][start : start + TOK_DEV, :] = ref[
                        :, columns_of(head * PER_GROUP + h)
                    ]


def stage(flags, table, query, out_grad):
    whole = pl.BlockSpec(memory_space=pltpu.VMEM)
    scalars = pl.BlockSpec(memory_space=pltpu.SMEM)
    shape = jax.ShapeDtypeStruct((HALF_KV * PER_GROUP * TOK_DEV, HEAD_WIDTH), jnp.bfloat16)
    outs = pl.pallas_call(
        stage_kernel,
        out_shape=[shape] * 4,
        in_specs=[scalars, scalars, whole, whole],
        out_specs=[whole] * 4,
        compiler_params=pltpu.CompilerParams(vmem_limit_bytes=VMEM_LIMIT),
        name="stage_rows",
    )(flags, table, query, out_grad)
    return outs[:2], outs[2:]


def attention_kernel(heavy, flags_ref, table_ref, q_ref, d_ref, *refs):
    chunks = 4 if heavy else 2
    mine, other = refs[:chunks], refs[chunks : 2 * chunks]
    cos_ref, sin_ref, low_ref = refs[2 * chunks : 2 * chunks + 3]
    before_ref = refs[2 * chunks + 3] if heavy else None
    gq_ref, term_ref, keep_ref, send_ref = refs[len(refs) - 9 : len(refs) - 5]
    k_all, v_all, low_all, dk_ref, dv_ref = refs[len(refs) - 5 :]
    sub = pl.program_id(0)
    odd, core = table_ref[0], table_ref[1]
    rows = 2 * TOK_DEV
    wide = PER_GROUP * TOK_DEV
    k_rows = pl.ds(pl.multiple_of(sub * TOK_DEV, TOK_DEV), TOK_DEV)
    v_rows = pl.ds(pl.multiple_of((2 + sub) * TOK_DEV, TOK_DEV), TOK_DEV)

    def branch(n):
        for j in range(n):
            for c, side in enumerate((mine[j], other[j])):
                span = slice(j * rows + c * TOK_DEV, j * rows + (c + 1) * TOK_DEV)
                k_all[span, :] = side[0, k_rows, :]
                v_all[span, :] = side[0, v_rows, :]
                low_all[:, span] = side[0, 4 * TOK_DEV :, :]
        width = n * rows
        key = lax.broadcasted_iota(jnp.int32, (rows, wide), 0)
        row = lax.broadcasted_iota(jnp.int32, (rows, wide), 1) % TOK_DEV
        limit = jnp.where(core == 1, rows, 0)
        allowed = (key <= row) | ((key >= TOK_DEV) & (key < limit))

        q = q_ref[...]
        d = d_ref[...]
        k = k_all[:width, :]
        s = lax.dot_general(k, q, NT, preferred_element_type=jnp.float32)
        near = jnp.where(allowed, s[:rows], MASKED)
        s = near if n == 1 else jnp.concatenate([near, s[rows:]], axis=0)
        dp = lax.dot_general(v_all[:width, :], d, NT, preferred_element_type=jnp.float32)
        top = jnp.max(s, axis=0, keepdims=True) * EXP2_SCALE
        p = jnp.exp2(s * EXP2_SCALE - top)
        inverse = 1.0 / jnp.sum(p, axis=0, keepdims=True)
        delta = jnp.sum(p * dp, axis=0, keepdims=True) * inverse
        p = p * inverse
        ds = (p * (dp - delta)).astype(jnp.bfloat16)
        dv_ref[:width, :] = jnp.dot(p.astype(jnp.bfloat16), d, preferred_element_type=jnp.float32)
        dk_ref[:width, :] = jnp.dot(ds, q, preferred_element_type=jnp.float32)
        dq = lax.dot_general(ds, k, TN, preferred_element_type=jnp.float32) * SCORE_SCALE
        low_rank = low_ref[...]
        parts = []
        for h in range(PER_GROUP):
            x = dq[h * TOK_DEV : (h + 1) * TOK_DEV, :]
            turned = x * cos_ref[...] + pltpu.roll(x, HEAD_WIDTH // 2, 1) * sin_ref[...]
            low = turned.astype(jnp.bfloat16)
            gq_ref[:, h * HEAD_WIDTH : (h + 1) * HEAD_WIDTH] = low
            parts.append(
                jnp.dot(low_rank, low, preferred_element_type=jnp.float32) * ADAPTER_SCALE
            )
        value_part = (
            jnp.dot(
                low_all[:, :width],
                dv_ref[:width, :].astype(jnp.bfloat16),
                preferred_element_type=jnp.float32,
            )
            * ADAPTER_SCALE
        )
        blank = jnp.zeros((TERM_ROWS - TERM_USED, HEAD_WIDTH), jnp.float32)
        for i in range(PER_GROUP // TERM_HEADS):
            these = slice(i * TERM_HEADS, (i + 1) * TERM_HEADS)
            block = jnp.concatenate([*parts[these], value_part[these], blank], axis=0)
            term_ref[i] = block.astype(jnp.bfloat16)

        def store(ref, j, span):
            for grad_ref, to_rows in ((dk_ref, k_rows), (dv_ref, v_rows)):
                if j < n:
                    grad = grad_ref[j * rows + span * TOK_DEV : j * rows + (span + 1) * TOK_DEV, :]
                else:
                    grad = jnp.zeros((TOK_DEV, HEAD_WIDTH), jnp.float32)
                ref[to_rows, :] = grad.astype(ref.dtype)

        first = 2 if heavy else 0
        for j in range(chunks):
            store(keep_ref.at[j], j, 0)
            store(send_ref.at[first + j], j, 1)

    if heavy:

        @pl.when(sub == 0)
        def _():
            send_ref[:2] = before_ref[...]

    base = 3 if heavy else 1
    for more in range(2):
        pl.when(odd == more)(lambda n=base + more: branch(n))


def attention(heavy, flags, table, rows, mine, other, cosine, sine, low, before):
    tok = TOK_DEV
    wide = PER_GROUP * HEAD_WIDTH
    chunks = len(mine)
    keys = chunks * 2 * tok
    place = 1 if heavy else 0

    def whole(shape):
        return pl.BlockSpec(shape, lambda s, f, t: (0,) * len(shape))

    def head(f, t, s):
        return head_of(f, t[2 + place], s)

    columns = pl.BlockSpec((tok, wide), lambda s, f, t: (0, head(f, t, s)))
    terms = pl.BlockSpec((PER_GROUP // TERM_HEADS, TERM_ROWS, HEAD_WIDTH), lambda s, f, t: (head(f, t, s), 0, 0))
    table_spec = whole((tok, HEAD_WIDTH))
    stacked = pl.BlockSpec((wide, HEAD_WIDTH), lambda s, f, t: (s, 0))
    in_specs = [stacked, stacked]
    for array, at in (*mine, *other):
        in_specs.append(
            pl.BlockSpec((1, PACK_ROWS, HEAD_WIDTH), lambda s, f, t, at=at: (at, 0, 0))
        )
    in_specs += [table_spec, table_spec, whole((RANK, tok))]
    operands = [*rows, *(array for array, at in (*mine, *other)), cosine, sine, low]
    aliases = {}
    if heavy:
        *before, light_send = before
        operands.append(light_send)
        in_specs.append(whole(light_send.shape))
        for out, array in enumerate(before):
            aliases[2 + len(operands)] = out
            operands.append(array)
            in_specs.append(pl.BlockSpec(memory_space=pl.ANY))
    out_shape = [
        jax.ShapeDtypeStruct((tok, QUERY_HEADS_HALF * HEAD_WIDTH), jnp.bfloat16),
        jax.ShapeDtypeStruct((PEERS, TERM_ROWS, HEAD_WIDTH), jnp.bfloat16),
        jax.ShapeDtypeStruct((chunks, 4 * tok, HEAD_WIDTH), jnp.float32),
        jax.ShapeDtypeStruct((6 if heavy else 2, 4 * tok, HEAD_WIDTH), jnp.bfloat16),
    ]
    return pl.pallas_call(
        partial(attention_kernel, heavy),
        grid_spec=pltpu.PrefetchScalarGridSpec(
            num_scalar_prefetch=2,
            grid=(HALF_KV,),
            in_specs=in_specs,
            out_specs=[columns, terms] + [whole(o.shape) for o in out_shape[2:]],
            scratch_shapes=[
                pltpu.VMEM((keys, HEAD_WIDTH), jnp.bfloat16),
                pltpu.VMEM((keys, HEAD_WIDTH), jnp.bfloat16),
                pltpu.VMEM((16, keys), jnp.bfloat16),
                pltpu.VMEM((keys, HEAD_WIDTH), jnp.float32),
                pltpu.VMEM((keys, HEAD_WIDTH), jnp.float32),
            ],
        ),
        out_shape=out_shape,
        input_output_aliases=aliases,
        compiler_params=pltpu.CompilerParams(
            dimension_semantics=("arbitrary",), vmem_limit_bytes=VMEM_LIMIT
        ),
        cost_estimate=pl.CostEstimate(
            flops=10 * HALF_KV * wide * keys * HEAD_WIDTH,
            bytes_accessed=6 << 20,
            transcendentals=HALF_KV * wide * keys,
        ),
        name="attention_heavy" if heavy else "attention_light",
    )(flags, table, *operands)


def finish_kernel(flags_ref, table_ref, cos_ref, sin_ref, *refs):
    light_keep, heavy_keep, light_from, heavy_from, side_ref, cross_ref, gk_ref, gv_ref = refs
    for place, (keep_ref, from_ref) in enumerate(
        ((light_keep, light_from), (heavy_keep, heavy_from))
    ):
        total = keep_ref[0] + from_ref[0].astype(jnp.float32) + side_ref[place].astype(jnp.float32)
        if place == 0:
            total += cross_ref[...].astype(jnp.float32)
        for sub in range(HALF_KV):
            columns = columns_of(head_of(flags_ref, table_ref[2 + place], sub))
            dk = total[sub * TOK_DEV : (sub + 1) * TOK_DEV] * SCORE_SCALE
            turned = dk * cos_ref[...] + pltpu.roll(dk, HEAD_WIDTH // 2, 1) * sin_ref[...]
            gk_ref[:, columns] = turned.astype(jnp.bfloat16)
            dv = total[(2 + sub) * TOK_DEV : (3 + sub) * TOK_DEV]
            gv_ref[:, columns] = dv.astype(jnp.bfloat16)


def finish(flags, table, cosine, sine, light_keep, heavy_keep, pair_from, side_back, cross_back):
    tok = TOK_DEV

    def whole(shape):
        return pl.BlockSpec(shape, lambda i, f, t: (0,) * len(shape))

    def block(at):
        return pl.BlockSpec((1, 4 * tok, HEAD_WIDTH), lambda i, f, t: (at, 0, 0))

    shape = jax.ShapeDtypeStruct((tok, KEY_VALUE_HEADS * HEAD_WIDTH), jnp.bfloat16)
    return pl.pallas_call(
        finish_kernel,
        grid_spec=pltpu.PrefetchScalarGridSpec(
            num_scalar_prefetch=2,
            grid=(1,),
            in_specs=[whole((tok, HEAD_WIDTH))] * 2
            + [block(0), block(0), block(0), block(2)]
            + [whole(side_back.shape), whole(cross_back.shape)],
            out_specs=[whole(shape.shape)] * 2,
        ),
        out_shape=[shape, shape],
        compiler_params=pltpu.CompilerParams(vmem_limit_bytes=VMEM_LIMIT),
        cost_estimate=pl.CostEstimate(
            flops=20_000_000_000, bytes_accessed=64 << 20, transcendentals=0
        ),
        name="finish_keys_values",
    )(flags, table, cosine, sine, light_keep, heavy_keep, pair_from, pair_from, side_back, cross_back)


def exchange(array, axes):
    return lax.all_to_all(array, axes, 0, 0)


def to_all(array, axes):
    count = lax.axis_size(axes)
    return exchange(jnp.broadcast_to(array[None], (count,) + array.shape), axes)


def add_up(array):
    return jnp.sum(array.astype(jnp.float32), axis=0).astype(jnp.bfloat16)


def local(query, keys, values, out_grad, query_lowrank_state, value_lowrank_state, shift_flags):
    ctx_index = lax.axis_index(SEQ_AXES)
    ctx_count = lax.axis_size(SEQ_AXES)

    def send(array, to):
        pairs = [(i, to(i) % ctx_count) for i in range(ctx_count) if to(i) is not None]
        return lax.ppermute(array, SEQ_AXES, pairs)

    def flip(mask):
        return lambda i: i ^ mask

    def to_odd(i):
        return i + 2 if i // 2 % 2 == 0 else None

    def to_even(i):
        return i - 2 if i // 2 % 2 == 1 else None

    chip = ctx_index // 2
    light_half = chip // 2 % 2
    table = jnp.stack([chip % 2, ctx_index % 2, light_half, 1 - light_half]).astype(jnp.int32)

    both, light = pack(shift_flags, table, keys[0], values[0], value_lowrank_state[0].T)
    crossed = send(light, lambda i: i + GROUP_DEV // 2)
    sided = send(both, to_odd)
    half_dim = HEAD_WIDTH // 2
    positions = ctx_index * TOK_DEV + jnp.arange(TOK_DEV, dtype=jnp.int32)
    inv_freq = 10000.0 ** (-(jnp.arange(half_dim, dtype=jnp.float32) * 2.0) / HEAD_WIDTH)
    angles = positions.astype(jnp.float32)[:, None] * inv_freq[None, :]
    cos_half, sin_half = jnp.cos(angles), jnp.sin(angles)
    cosine = jnp.concatenate([cos_half, cos_half], axis=1)
    sine = jnp.concatenate([sin_half, -sin_half], axis=1)
    low = query_lowrank_state[0].T
    light_rows, heavy_rows = stage(shift_flags, table, query[0], out_grad[0])
    crossed, sided, cosine, sine, low, light_rows, heavy_rows = lax.optimization_barrier(
        (crossed, sided, cosine, sine, low, light_rows, heavy_rows)
    )
    crossed = crossed[None]
    swapped = send(crossed, flip(2))
    arrived = send(jnp.concatenate([both, sided, crossed]), flip(1))
    swapped_other = send(crossed, flip(3))
    gq, terms, light_keep, light_send = attention(
        False, shift_flags, table, light_rows,
        [(both, 0), (sided, 0)], [(arrived, 0), (arrived, 2)],
        cosine, sine, low, None,
    )
    gq, terms, heavy_keep, pair_send = attention(
        True, shift_flags, table, heavy_rows,
        [(both, 1), (crossed, 0), (swapped, 0), (sided, 1)],
        [(arrived, 1), (arrived, 4), (swapped_other, 0), (arrived, 3)],
        cosine, sine, low, (gq, terms, light_send),
    )

    def wide(array):
        return array.astype(jnp.float32)

    def sent(array):
        return array.astype(jnp.bfloat16)

    terms = exchange(terms, "zc")
    pair_from = send(pair_send, flip(1))
    swap_from = send(sent(heavy_keep[2] + wide(pair_from[4])), flip(2))
    terms, pair_from, swap_from = lax.optimization_barrier((terms, pair_from, swap_from))
    cross_back = send(
        sent(heavy_keep[1] + wide(pair_from[3]) + wide(swap_from)), lambda i: i - GROUP_DEV // 2
    )
    side_back = send(
        sent(jnp.stack([light_keep[1] + wide(pair_from[1]), heavy_keep[3] + wide(pair_from[5])])),
        to_even,
    )
    terms = to_all(add_up(terms)[:TERM_USED], SUM_AXES)
    gk, gv = finish(
        shift_flags, table, cosine, sine, light_keep, heavy_keep, pair_from, side_back, cross_back
    )
    terms = to_all(add_up(terms), "zc")
    query_terms = terms[:, : TERM_HEADS * RANK].reshape(QUERY_HEADS_HALF, RANK, HEAD_WIDTH)
    value_terms = terms[:, TERM_HEADS * RANK :].reshape(KEY_VALUE_HEADS, RANK, HEAD_WIDTH)

    def rank_rows(heads):
        return wide(jnp.transpose(heads, (1, 0, 2)).reshape(RANK, -1))

    return gq[None], gk[None], gv[None], rank_rows(query_terms), rank_rows(value_terms)


def solution(mesh):
    dp, ctx = mesh.shape["dp"], mesh.shape["ctx"]
    split = Mesh(mesh.devices.reshape(dp, ctx // PEERS, PEERS), ("dp", "yh", "zc"))
    rows = P("dp", SEQ_AXES, None)
    return jax.shard_map(
        local,
        mesh=split,
        in_specs=(rows,) * 6 + (P(),),
        out_specs=(rows, rows, rows, P(), P()),
        check_vma=False,
    )
```

```python
from functools import partial
import math

import jax
import jax.numpy as jnp
from jax import lax
from jax.experimental import pallas as pl
from jax.experimental.pallas import tpu as pltpu
from jax.sharding import Mesh, PartitionSpec as P

QUERY_HEADS_HALF = 32
KEY_VALUE_HEADS = 4
HEAD_WIDTH = 128
GROUP_DEV = 8
TOK_DEV = 128
HALF_KV = KEY_VALUE_HEADS // 2
PER_GROUP = QUERY_HEADS_HALF // KEY_VALUE_HEADS
RANK = 8
PACK_ROWS = 4 * TOK_DEV + 16
PEERS = 16
TERM_ROWS = 32
TERM_HEADS = QUERY_HEADS_HALF // PEERS
TERM_USED = TERM_HEADS * (RANK + 1)
ADAPTER_SCALE = 2.0
SCORE_SCALE = 1.0 / math.sqrt(HEAD_WIDTH)
EXP2_SCALE = SCORE_SCALE * math.log2(math.e)
MASKED = -1e30
NT = (((1,), (1,)), ((), ()))
TN = (((0,), (0,)), ((), ()))
VMEM_LIMIT = 20 * 1024 * 1024
SEQ_AXES = ("yh", "zc")
SUM_AXES = ("dp", "yh")


def head_of(flags, half, sub):
    hit = [flags[head] == half for head in range(KEY_VALUE_HEADS)]
    low = jnp.where(hit[0], 0, jnp.where(hit[1], 1, 2))
    high = jnp.where(hit[3], 3, jnp.where(hit[2], 2, 1))
    return jnp.where(sub == 0, low, high)


def columns_of(head):
    return pl.ds(pl.multiple_of(head * HEAD_WIDTH, HEAD_WIDTH), HEAD_WIDTH)


def pack_kernel(flags_ref, keys_ref, values_ref, low_ref, both_ref, light_ref):
    light_half = lax.axis_index("zc") // 4 % 2
    low = low_ref[...].astype(jnp.float32)
    low = jnp.concatenate([low, jnp.zeros_like(low)], axis=0).astype(jnp.bfloat16)
    for place in range(2):
        half = 1 - light_half if place else light_half
        for sub in range(HALF_KV):
            columns = columns_of(head_of(flags_ref, half, sub))
            for kind, ref in enumerate((keys_ref, values_ref)):
                rows = slice((2 * kind + sub) * TOK_DEV, (2 * kind + sub + 1) * TOK_DEV)
                both_ref[place, rows, :] = ref[:, columns]
                if place == 0:
                    light_ref[rows, :] = ref[:, columns]
        both_ref[place, 4 * TOK_DEV :, :] = low
    light_ref[4 * TOK_DEV :, :] = low


def pack(flags, keys, values, low):
    whole = pl.BlockSpec(memory_space=pltpu.VMEM)
    scalars = pl.BlockSpec(memory_space=pltpu.SMEM)
    return pl.pallas_call(
        pack_kernel,
        out_shape=(
            jax.ShapeDtypeStruct((2, PACK_ROWS, HEAD_WIDTH), jnp.bfloat16),
            jax.ShapeDtypeStruct((PACK_ROWS, HEAD_WIDTH), jnp.bfloat16),
        ),
        in_specs=[scalars, whole, whole, whole],
        out_specs=(whole, whole),
        name="pack_heads",
    )(flags, keys, values, low)


def stage_kernel(flags_ref, table_ref, query_ref, out_grad_ref, *outs):
    for place in range(2):
        for sub in range(HALF_KV):
            head = head_of(flags_ref, table_ref[2 + place], sub)
            for h in range(PER_GROUP):
                start = (sub * PER_GROUP + h) * TOK_DEV
                for kind, ref in enumerate((query_ref, out_grad_ref)):
                    outs[2 * place + kind][start : start + TOK_DEV, :] = ref[
                        :, columns_of(head * PER_GROUP + h)
                    ]


def stage(flags, table, query, out_grad):
    whole = pl.BlockSpec(memory_space=pltpu.VMEM)
    scalars = pl.BlockSpec(memory_space=pltpu.SMEM)
    shape = jax.ShapeDtypeStruct((HALF_KV * PER_GROUP * TOK_DEV, HEAD_WIDTH), jnp.bfloat16)
    outs = pl.pallas_call(
        stage_kernel,
        out_shape=[shape] * 4,
        in_specs=[scalars, scalars, whole, whole],
        out_specs=[whole] * 4,
        compiler_params=pltpu.CompilerParams(vmem_limit_bytes=VMEM_LIMIT),
        name="stage_rows",
    )(flags, table, query, out_grad)
    return outs[:2], outs[2:]


def attention_kernel(heavy, flags_ref, table_ref, q_ref, d_ref, *refs):
    chunks = 4 if heavy else 2
    mine, other = refs[:chunks], refs[chunks : 2 * chunks]
    cos_ref, sin_ref, low_ref = refs[2 * chunks : 2 * chunks + 3]
    before_ref = refs[2 * chunks + 3] if heavy else None
    gq_ref, term_ref, keep_ref, send_ref = refs[len(refs) - 9 : len(refs) - 5]
    k_all, v_all, low_all, dk_ref, dv_ref = refs[len(refs) - 5 :]
    sub = pl.program_id(0)
    odd, core = table_ref[0], table_ref[1]
    rows = 2 * TOK_DEV
    wide = PER_GROUP * TOK_DEV
    k_rows = pl.ds(pl.multiple_of(sub * TOK_DEV, TOK_DEV), TOK_DEV)
    v_rows = pl.ds(pl.multiple_of((2 + sub) * TOK_DEV, TOK_DEV), TOK_DEV)

    def branch(n):
        for j in range(n):
            for c, side in enumerate((mine[j], other[j])):
                span = slice(j * rows + c * TOK_DEV, j * rows + (c + 1) * TOK_DEV)
                k_all[span, :] = side[0, k_rows, :]
                v_all[span, :] = side[0, v_rows, :]
                low_all[:, span] = side[0, 4 * TOK_DEV :, :]
        width = n * rows
        key = lax.broadcasted_iota(jnp.int32, (rows, wide), 0)
        row = lax.broadcasted_iota(jnp.int32, (rows, wide), 1) % TOK_DEV
        limit = jnp.where(core == 1, rows, 0)
        allowed = (key <= row) | ((key >= TOK_DEV) & (key < limit))

        q = q_ref[...]
        d = d_ref[...]
        k = k_all[:width, :]
        s = lax.dot_general(k, q, NT, preferred_element_type=jnp.float32)
        near = jnp.where(allowed, s[:rows], MASKED)
        s = near if n == 1 else jnp.concatenate([near, s[rows:]], axis=0)
        dp = lax.dot_general(v_all[:width, :], d, NT, preferred_element_type=jnp.float32)
        top = jnp.max(s, axis=0, keepdims=True) * EXP2_SCALE
        p = jnp.exp2(s * EXP2_SCALE - top)
        inverse = 1.0 / jnp.sum(p, axis=0, keepdims=True)
        delta = jnp.sum(p * dp, axis=0, keepdims=True) * inverse
        p = p * inverse
        ds = (p * (dp - delta)).astype(jnp.bfloat16)
        dv_ref[:width, :] = jnp.dot(p.astype(jnp.bfloat16), d, preferred_element_type=jnp.float32)
        dk_ref[:width, :] = jnp.dot(ds, q, preferred_element_type=jnp.float32)
        dq = lax.dot_general(ds, k, TN, preferred_element_type=jnp.float32) * SCORE_SCALE
        low_rank = low_ref[...]
        parts = []
        for h in range(PER_GROUP):
            x = dq[h * TOK_DEV : (h + 1) * TOK_DEV, :]
            turned = x * cos_ref[...] + pltpu.roll(x, HEAD_WIDTH // 2, 1) * sin_ref[...]
            low = turned.astype(jnp.bfloat16)
            gq_ref[:, h * HEAD_WIDTH : (h + 1) * HEAD_WIDTH] = low
            parts.append(
                jnp.dot(low_rank, low, preferred_element_type=jnp.float32) * ADAPTER_SCALE
            )
        value_part = (
            jnp.dot(
                low_all[:, :width],
                dv_ref[:width, :].astype(jnp.bfloat16),
                preferred_element_type=jnp.float32,
            )
            * ADAPTER_SCALE
        )
        blank = jnp.zeros((TERM_ROWS - TERM_USED, HEAD_WIDTH), jnp.float32)
        for i in range(PER_GROUP // TERM_HEADS):
            these = slice(i * TERM_HEADS, (i + 1) * TERM_HEADS)
            block = jnp.concatenate([*parts[these], value_part[these], blank], axis=0)
            term_ref[i] = block.astype(jnp.bfloat16)

        def store(ref, j, span):
            for grad_ref, to_rows in ((dk_ref, k_rows), (dv_ref, v_rows)):
                if j < n:
                    grad = grad_ref[j * rows + span * TOK_DEV : j * rows + (span + 1) * TOK_DEV, :]
                else:
                    grad = jnp.zeros((TOK_DEV, HEAD_WIDTH), jnp.float32)
                ref[to_rows, :] = grad.astype(ref.dtype)

        first = 2 if heavy else 0
        for j in range(chunks):
            store(keep_ref.at[j], j, 0)
            store(send_ref.at[first + j], j, 1)

    if heavy:

        @pl.when(sub == 0)
        def _():
            send_ref[:2] = before_ref[...]

    base = 3 if heavy else 1
    for more in range(2):
        pl.when(odd == more)(lambda n=base + more: branch(n))


def attention(heavy, flags, table, rows, mine, other, cosine, sine, low, before):
    tok = TOK_DEV
    wide = PER_GROUP * HEAD_WIDTH
    chunks = len(mine)
    keys = chunks * 2 * tok
    place = 1 if heavy else 0

    def whole(shape):
        return pl.BlockSpec(shape, lambda s, f, t: (0,) * len(shape))

    def head(f, t, s):
        return head_of(f, t[2 + place], s)

    columns = pl.BlockSpec((tok, wide), lambda s, f, t: (0, head(f, t, s)))
    terms = pl.BlockSpec((PER_GROUP // TERM_HEADS, TERM_ROWS, HEAD_WIDTH), lambda s, f, t: (head(f, t, s), 0, 0))
    table_spec = whole((tok, HEAD_WIDTH))
    stacked = pl.BlockSpec((wide, HEAD_WIDTH), lambda s, f, t: (s, 0))
    in_specs = [stacked, stacked]
    for array, at in (*mine, *other):
        in_specs.append(
            pl.BlockSpec((1, PACK_ROWS, HEAD_WIDTH), lambda s, f, t, at=at: (at, 0, 0))
        )
    in_specs += [table_spec, table_spec, whole((RANK, tok))]
    operands = [*rows, *(array for array, at in (*mine, *other)), cosine, sine, low]
    aliases = {}
    if heavy:
        *before, light_send = before
        operands.append(light_send)
        in_specs.append(whole(light_send.shape))
        for out, array in enumerate(before):
            aliases[2 + len(operands)] = out
            operands.append(array)
            in_specs.append(pl.BlockSpec(memory_space=pl.ANY))
    out_shape = [
        jax.ShapeDtypeStruct((tok, QUERY_HEADS_HALF * HEAD_WIDTH), jnp.bfloat16),
        jax.ShapeDtypeStruct((PEERS, TERM_ROWS, HEAD_WIDTH), jnp.bfloat16),
        jax.ShapeDtypeStruct((chunks, 4 * tok, HEAD_WIDTH), jnp.float32),
        jax.ShapeDtypeStruct((6 if heavy else 2, 4 * tok, HEAD_WIDTH), jnp.bfloat16),
    ]
    return pl.pallas_call(
        partial(attention_kernel, heavy),
        grid_spec=pltpu.PrefetchScalarGridSpec(
            num_scalar_prefetch=2,
            grid=(HALF_KV,),
            in_specs=in_specs,
            out_specs=[columns, terms] + [whole(o.shape) for o in out_shape[2:]],
            scratch_shapes=[
                pltpu.VMEM((keys, HEAD_WIDTH), jnp.bfloat16),
                pltpu.VMEM((keys, HEAD_WIDTH), jnp.bfloat16),
                pltpu.VMEM((16, keys), jnp.bfloat16),
                pltpu.VMEM((keys, HEAD_WIDTH), jnp.float32),
                pltpu.VMEM((keys, HEAD_WIDTH), jnp.float32),
            ],
        ),
        out_shape=out_shape,
        input_output_aliases=aliases,
        compiler_params=pltpu.CompilerParams(
            dimension_semantics=("arbitrary",), vmem_limit_bytes=VMEM_LIMIT
        ),
        cost_estimate=pl.CostEstimate(
            flops=10 * HALF_KV * wide * keys * HEAD_WIDTH,
            bytes_accessed=6 << 20,
            transcendentals=HALF_KV * wide * keys,
        ),
        name="attention_heavy" if heavy else "attention_light",
    )(flags, table, *operands)


def finish_kernel(flags_ref, table_ref, cos_ref, sin_ref, *refs):
    light_keep, heavy_keep, light_from, heavy_from, side_ref, cross_ref, gk_ref, gv_ref = refs
    for place, (keep_ref, from_ref) in enumerate(
        ((light_keep, light_from), (heavy_keep, heavy_from))
    ):
        total = keep_ref[0] + from_ref[0].astype(jnp.float32) + side_ref[place].astype(jnp.float32)
        if place == 0:
            total += cross_ref[...].astype(jnp.float32)
        for sub in range(HALF_KV):
            columns = columns_of(head_of(flags_ref, table_ref[2 + place], sub))
            dk = total[sub * TOK_DEV : (sub + 1) * TOK_DEV] * SCORE_SCALE
            turned = dk * cos_ref[...] + pltpu.roll(dk, HEAD_WIDTH // 2, 1) * sin_ref[...]
            gk_ref[:, columns] = turned.astype(jnp.bfloat16)
            dv = total[(2 + sub) * TOK_DEV : (3 + sub) * TOK_DEV]
            gv_ref[:, columns] = dv.astype(jnp.bfloat16)


def finish(flags, table, cosine, sine, light_keep, heavy_keep, pair_from, side_back, cross_back):
    tok = TOK_DEV

    def whole(shape):
        return pl.BlockSpec(shape, lambda i, f, t: (0,) * len(shape))

    def block(at):
        return pl.BlockSpec((1, 4 * tok, HEAD_WIDTH), lambda i, f, t: (at, 0, 0))

    shape = jax.ShapeDtypeStruct((tok, KEY_VALUE_HEADS * HEAD_WIDTH), jnp.bfloat16)
    return pl.pallas_call(
        finish_kernel,
        grid_spec=pltpu.PrefetchScalarGridSpec(
            num_scalar_prefetch=2,
            grid=(1,),
            in_specs=[whole((tok, HEAD_WIDTH))] * 2
            + [block(0), block(0), block(0), block(2)]
            + [whole(side_back.shape), whole(cross_back.shape)],
            out_specs=[whole(shape.shape)] * 2,
        ),
        out_shape=[shape, shape],
        compiler_params=pltpu.CompilerParams(vmem_limit_bytes=VMEM_LIMIT),
        cost_estimate=pl.CostEstimate(
            flops=20_000_000_000, bytes_accessed=64 << 20, transcendentals=0
        ),
        name="finish_keys_values",
    )(flags, table, cosine, sine, light_keep, heavy_keep, pair_from, pair_from, side_back, cross_back)


def exchange(array, axes):
    return lax.all_to_all(array, axes, 0, 0)


def to_all(array, axes):
    count = lax.axis_size(axes)
    return exchange(jnp.broadcast_to(array[None], (count,) + array.shape), axes)


def add_up(array):
    return jnp.sum(array.astype(jnp.float32), axis=0).astype(jnp.bfloat16)


def local(query, keys, values, out_grad, query_lowrank_state, value_lowrank_state, shift_flags):
    ctx_index = lax.axis_index(SEQ_AXES)
    ctx_count = lax.axis_size(SEQ_AXES)

    def send(array, to):
        pairs = [(i, to(i) % ctx_count) for i in range(ctx_count) if to(i) is not None]
        return lax.ppermute(array, SEQ_AXES, pairs)

    def flip(mask):
        return lambda i: i ^ mask

    def to_odd(i):
        return i + 2 if i // 2 % 2 == 0 else None

    def to_even(i):
        return i - 2 if i // 2 % 2 == 1 else None

    chip = ctx_index // 2
    light_half = chip // 2 % 2
    table = jnp.stack([chip % 2, ctx_index % 2, light_half, 1 - light_half]).astype(jnp.int32)

    both, light = pack(shift_flags, keys[0], values[0], value_lowrank_state[0].T)
    crossed = send(light, lambda i: i + GROUP_DEV // 2)
    sided = send(both, to_odd)
    half_dim = HEAD_WIDTH // 2
    positions = ctx_index * TOK_DEV + jnp.arange(TOK_DEV, dtype=jnp.int32)
    inv_freq = 10000.0 ** (-(jnp.arange(half_dim, dtype=jnp.float32) * 2.0) / HEAD_WIDTH)
    angles = positions.astype(jnp.float32)[:, None] * inv_freq[None, :]
    cos_half, sin_half = jnp.cos(angles), jnp.sin(angles)
    cosine = jnp.concatenate([cos_half, cos_half], axis=1)
    sine = jnp.concatenate([sin_half, -sin_half], axis=1)
    low = query_lowrank_state[0].T
    light_rows, heavy_rows = stage(shift_flags, table, query[0], out_grad[0])
    crossed, sided, cosine, sine, low, light_rows, heavy_rows = lax.optimization_barrier(
        (crossed, sided, cosine, sine, low, light_rows, heavy_rows)
    )
    crossed = crossed[None]
    swapped = send(crossed, flip(2))
    arrived = send(jnp.concatenate([both, sided, crossed]), flip(1))
    swapped_other = send(crossed, flip(3))
    gq, terms, light_keep, light_send = attention(
        False, shift_flags, table, light_rows,
        [(both, 0), (sided, 0)], [(arrived, 0), (arrived, 2)],
        cosine, sine, low, None,
    )
    gq, terms, heavy_keep, pair_send = attention(
        True, shift_flags, table, heavy_rows,
        [(both, 1), (crossed, 0), (swapped, 0), (sided, 1)],
        [(arrived, 1), (arrived, 4), (swapped_other, 0), (arrived, 3)],
        cosine, sine, low, (gq, terms, light_send),
    )

    def wide(array):
        return array.astype(jnp.float32)

    def sent(array):
        return array.astype(jnp.bfloat16)

    terms = exchange(terms, "zc")
    pair_from = send(pair_send, flip(1))
    swap_from = send(sent(heavy_keep[2] + wide(pair_from[4])), flip(2))
    terms, pair_from, swap_from = lax.optimization_barrier((terms, pair_from, swap_from))
    cross_back = send(
        sent(heavy_keep[1] + wide(pair_from[3]) + wide(swap_from)), lambda i: i - GROUP_DEV // 2
    )
    side_back = send(
        sent(jnp.stack([light_keep[1] + wide(pair_from[1]), heavy_keep[3] + wide(pair_from[5])])),
        to_even,
    )
    terms = to_all(add_up(terms)[:TERM_USED], SUM_AXES)
    gk, gv = finish(
        shift_flags, table, cosine, sine, light_keep, heavy_keep, pair_from, side_back, cross_back
    )
    terms = to_all(add_up(terms), "zc")
    query_terms = terms[:, : TERM_HEADS * RANK].reshape(QUERY_HEADS_HALF, RANK, HEAD_WIDTH)
    value_terms = terms[:, TERM_HEADS * RANK :].reshape(KEY_VALUE_HEADS, RANK, HEAD_WIDTH)

    def rank_rows(heads):
        return wide(jnp.transpose(heads, (1, 0, 2)).reshape(RANK, -1))

    return gq[None], gk[None], gv[None], rank_rows(query_terms), rank_rows(value_terms)


def solution(mesh):
    dp, ctx = mesh.shape["dp"], mesh.shape["ctx"]
    split = Mesh(mesh.devices.reshape(dp, ctx // PEERS, PEERS), ("dp", "yh", "zc"))
    rows = P("dp", SEQ_AXES, None)
    return jax.shard_map(
        local,
        mesh=split,
        in_specs=(rows,) * 6 + (P(),),
        out_specs=(rows, rows, rows, P(), P()),
        check_vma=False,
    )
```

```python
from functools import partial
import math

import jax
import jax.numpy as jnp
from jax import lax
from jax.experimental import pallas as pl
from jax.experimental.pallas import tpu as pltpu
from jax.sharding import Mesh, PartitionSpec as P

QUERY_HEADS_HALF = 32
KEY_VALUE_HEADS = 4
HEAD_WIDTH = 128
GROUP_DEV = 8
TOK_DEV = 128
HALF_KV = KEY_VALUE_HEADS // 2
PER_GROUP = QUERY_HEADS_HALF // KEY_VALUE_HEADS
RANK = 8
PACK_ROWS = 4 * TOK_DEV + 16
PEERS = 16
TERM_ROWS = 32
TERM_HEADS = QUERY_HEADS_HALF // PEERS
TERM_USED = TERM_HEADS * (RANK + 1)
ADAPTER_SCALE = 2.0
SCORE_SCALE = 1.0 / math.sqrt(HEAD_WIDTH)
EXP2_SCALE = SCORE_SCALE * math.log2(math.e)
MASKED = -1e30
NT = (((1,), (1,)), ((), ()))
TN = (((0,), (0,)), ((), ()))
VMEM_LIMIT = 20 * 1024 * 1024
SEQ_AXES = ("yh", "zc")
SUM_AXES = ("dp", "yh")


def head_of(flags, half, sub):
    hit = [flags[head] == half for head in range(KEY_VALUE_HEADS)]
    low = jnp.where(hit[0], 0, jnp.where(hit[1], 1, 2))
    high = jnp.where(hit[3], 3, jnp.where(hit[2], 2, 1))
    return jnp.where(sub == 0, low, high)


def columns_of(head):
    return pl.ds(pl.multiple_of(head * HEAD_WIDTH, HEAD_WIDTH), HEAD_WIDTH)


def pack_kernel(flags_ref, keys_ref, values_ref, low_ref, both_ref, light_ref):
    light_half = lax.axis_index("zc") // 4 % 2
    low = low_ref[...].astype(jnp.float32)
    low = jnp.concatenate([low, jnp.zeros_like(low)], axis=0).astype(jnp.bfloat16)
    for place in range(2):
        half = 1 - light_half if place else light_half
        for sub in range(HALF_KV):
            columns = columns_of(head_of(flags_ref, half, sub))
            for kind, ref in enumerate((keys_ref, values_ref)):
                rows = slice((2 * kind + sub) * TOK_DEV, (2 * kind + sub + 1) * TOK_DEV)
                both_ref[place, rows, :] = ref[:, columns]
                if place == 0:
                    light_ref[rows, :] = ref[:, columns]
        both_ref[place, 4 * TOK_DEV :, :] = low
    light_ref[4 * TOK_DEV :, :] = low


def pack(flags, keys, values, low):
    whole = pl.BlockSpec(memory_space=pltpu.VMEM)
    scalars = pl.BlockSpec(memory_space=pltpu.SMEM)
    return pl.pallas_call(
        pack_kernel,
        out_shape=(
            jax.ShapeDtypeStruct((2, PACK_ROWS, HEAD_WIDTH), jnp.bfloat16),
            jax.ShapeDtypeStruct((PACK_ROWS, HEAD_WIDTH), jnp.bfloat16),
        ),
        in_specs=[scalars, whole, whole, whole],
        out_specs=(whole, whole),
        name="pack_heads",
    )(flags, keys, values, low)


def stage_kernel(flags_ref, table_ref, query_ref, out_grad_ref, *outs):
    for place in range(2):
        for sub in range(HALF_KV):
            head = head_of(flags_ref, table_ref[2 + place], sub)
            for h in range(PER_GROUP):
                start = (sub * PER_GROUP + h) * TOK_DEV
                for kind, ref in enumerate((query_ref, out_grad_ref)):
                    outs[2 * place + kind][start : start + TOK_DEV, :] = ref[
                        :, columns_of(head * PER_GROUP + h)
                    ]


def stage(flags, table, query, out_grad):
    whole = pl.BlockSpec(memory_space=pltpu.VMEM)
    scalars = pl.BlockSpec(memory_space=pltpu.SMEM)
    shape = jax.ShapeDtypeStruct((HALF_KV * PER_GROUP * TOK_DEV, HEAD_WIDTH), jnp.bfloat16)
    outs = pl.pallas_call(
        stage_kernel,
        out_shape=[shape] * 4,
        in_specs=[scalars, scalars, whole, whole],
        out_specs=[whole] * 4,
        compiler_params=pltpu.CompilerParams(vmem_limit_bytes=VMEM_LIMIT),
        name="stage_rows",
    )(flags, table, query, out_grad)
    return outs[:2], outs[2:]


def attention_kernel(heavy, flags_ref, table_ref, q_ref, d_ref, *refs):
    chunks = 4 if heavy else 2
    mine, other = refs[:chunks], refs[chunks : 2 * chunks]
    cos_ref, sin_ref, low_ref = refs[2 * chunks : 2 * chunks + 3]
    before_ref = refs[2 * chunks + 3] if heavy else None
    gq_ref, term_ref, keep_ref, send_ref = refs[len(refs) - 9 : len(refs) - 5]
    k_all, v_all, low_all, dk_ref, dv_ref = refs[len(refs) - 5 :]
    sub = pl.program_id(0)
    odd, core = table_ref[0], table_ref[1]
    rows = 2 * TOK_DEV
    tiles = 1 if heavy else 2
    part = PER_GROUP * TOK_DEV // tiles
    k_rows = pl.ds(pl.multiple_of(sub * TOK_DEV, TOK_DEV), TOK_DEV)
    v_rows = pl.ds(pl.multiple_of((2 + sub) * TOK_DEV, TOK_DEV), TOK_DEV)

    def branch(n):
        for j in range(n):
            for c, side in enumerate((mine[j], other[j])):
                span = slice(j * rows + c * TOK_DEV, j * rows + (c + 1) * TOK_DEV)
                k_all[span, :] = side[0, k_rows, :]
                v_all[span, :] = side[0, v_rows, :]
                low_all[:, span] = side[0, 4 * TOK_DEV :, :]
        width = n * rows
        key = lax.broadcasted_iota(jnp.int32, (rows, part), 0)
        row = lax.broadcasted_iota(jnp.int32, (rows, part), 1) % TOK_DEV
        limit = jnp.where(core == 1, rows, 0)
        allowed = (key <= row) | ((key >= TOK_DEV) & (key < limit))

        k = k_all[:width, :]
        v = v_all[:width, :]

        def products(t):
            q, d = (ref[t * part : (t + 1) * part, :] for ref in (q_ref, d_ref))
            s = lax.dot_general(k, q, NT, preferred_element_type=jnp.float32)
            near = jnp.where(allowed, s[:rows], MASKED)
            s = near if n == 1 else jnp.concatenate([near, s[rows:]], axis=0)
            dp = lax.dot_general(v, d, NT, preferred_element_type=jnp.float32)
            top = jnp.max(s, axis=0, keepdims=True) * EXP2_SCALE
            p = jnp.exp2(s * EXP2_SCALE - top)
            inverse = 1.0 / jnp.sum(p, axis=0, keepdims=True)
            delta = jnp.sum(p * dp, axis=0, keepdims=True) * inverse
            p = p * inverse
            ds = (p * (dp - delta)).astype(jnp.bfloat16)
            return q, d, p.astype(jnp.bfloat16), ds

        dqs = []
        ahead = products(0)
        for t in range(tiles):
            q, d, p, ds = ahead
            if t + 1 < tiles:
                ahead = products(t + 1)
            dv = jnp.dot(p, d, preferred_element_type=jnp.float32)
            dk = jnp.dot(ds, q, preferred_element_type=jnp.float32)
            if t == 0:
                dv_ref[:width, :] = dv
                dk_ref[:width, :] = dk
            else:
                dv_ref[:width, :] += dv
                dk_ref[:width, :] += dk
            dqs.append(lax.dot_general(ds, k, TN, preferred_element_type=jnp.float32))
        dq = jnp.concatenate(dqs, axis=0) * SCORE_SCALE
        low_rank = low_ref[...]
        parts = []
        for h in range(PER_GROUP):
            x = dq[h * TOK_DEV : (h + 1) * TOK_DEV, :]
            turned = x * cos_ref[...] + pltpu.roll(x, HEAD_WIDTH // 2, 1) * sin_ref[...]
            low = turned.astype(jnp.bfloat16)
            gq_ref[:, h * HEAD_WIDTH : (h + 1) * HEAD_WIDTH] = low
            parts.append(
                jnp.dot(low_rank, low, preferred_element_type=jnp.float32) * ADAPTER_SCALE
            )
        value_part = (
            jnp.dot(
                low_all[:, :width],
                dv_ref[:width, :].astype(jnp.bfloat16),
                preferred_element_type=jnp.float32,
            )
            * ADAPTER_SCALE
        )
        blank = jnp.zeros((TERM_ROWS - TERM_USED, HEAD_WIDTH), jnp.float32)
        for i in range(PER_GROUP // TERM_HEADS):
            these = slice(i * TERM_HEADS, (i + 1) * TERM_HEADS)
            block = jnp.concatenate([*parts[these], value_part[these], blank], axis=0)
            term_ref[i] = block.astype(jnp.bfloat16)

        def store(ref, j, span):
            for grad_ref, to_rows in ((dk_ref, k_rows), (dv_ref, v_rows)):
                if j < n:
                    grad = grad_ref[j * rows + span * TOK_DEV : j * rows + (span + 1) * TOK_DEV, :]
                else:
                    grad = jnp.zeros((TOK_DEV, HEAD_WIDTH), jnp.float32)
                ref[to_rows, :] = grad.astype(ref.dtype)

        first = 2 if heavy else 0
        for j in range(chunks):
            store(keep_ref.at[j], j, 0)
            store(send_ref.at[first + j], j, 1)

    if heavy:

        @pl.when(sub == 0)
        def _():
            send_ref[:2] = before_ref[...]

    base = 3 if heavy else 1
    for more in range(2):
        pl.when(odd == more)(lambda n=base + more: branch(n))


def attention(heavy, flags, table, rows, mine, other, cosine, sine, low, before):
    tok = TOK_DEV
    wide = PER_GROUP * HEAD_WIDTH
    chunks = len(mine)
    keys = chunks * 2 * tok
    place = 1 if heavy else 0

    def whole(shape):
        return pl.BlockSpec(shape, lambda s, f, t: (0,) * len(shape))

    def head(f, t, s):
        return head_of(f, t[2 + place], s)

    columns = pl.BlockSpec((tok, wide), lambda s, f, t: (0, head(f, t, s)))
    terms = pl.BlockSpec((PER_GROUP // TERM_HEADS, TERM_ROWS, HEAD_WIDTH), lambda s, f, t: (head(f, t, s), 0, 0))
    table_spec = whole((tok, HEAD_WIDTH))
    stacked = pl.BlockSpec((wide, HEAD_WIDTH), lambda s, f, t: (s, 0))
    in_specs = [stacked, stacked]
    for array, at in (*mine, *other):
        in_specs.append(
            pl.BlockSpec((1, PACK_ROWS, HEAD_WIDTH), lambda s, f, t, at=at: (at, 0, 0))
        )
    in_specs += [table_spec, table_spec, whole((RANK, tok))]
    operands = [*rows, *(array for array, at in (*mine, *other)), cosine, sine, low]
    aliases = {}
    if heavy:
        *before, light_send = before
        operands.append(light_send)
        in_specs.append(whole(light_send.shape))
        for out, array in enumerate(before):
            aliases[2 + len(operands)] = out
            operands.append(array)
            in_specs.append(pl.BlockSpec(memory_space=pl.ANY))
    out_shape = [
        jax.ShapeDtypeStruct((tok, QUERY_HEADS_HALF * HEAD_WIDTH), jnp.bfloat16),
        jax.ShapeDtypeStruct((PEERS, TERM_ROWS, HEAD_WIDTH), jnp.bfloat16),
        jax.ShapeDtypeStruct((chunks, 4 * tok, HEAD_WIDTH), jnp.float32),
        jax.ShapeDtypeStruct((6 if heavy else 2, 4 * tok, HEAD_WIDTH), jnp.bfloat16),
    ]
    return pl.pallas_call(
        partial(attention_kernel, heavy),
        grid_spec=pltpu.PrefetchScalarGridSpec(
            num_scalar_prefetch=2,
            grid=(HALF_KV,),
            in_specs=in_specs,
            out_specs=[columns, terms] + [whole(o.shape) for o in out_shape[2:]],
            scratch_shapes=[
                pltpu.VMEM((keys, HEAD_WIDTH), jnp.bfloat16),
                pltpu.VMEM((keys, HEAD_WIDTH), jnp.bfloat16),
                pltpu.VMEM((16, keys), jnp.bfloat16),
                pltpu.VMEM((keys, HEAD_WIDTH), jnp.float32),
                pltpu.VMEM((keys, HEAD_WIDTH), jnp.float32),
            ],
        ),
        out_shape=out_shape,
        input_output_aliases=aliases,
        compiler_params=pltpu.CompilerParams(
            dimension_semantics=("arbitrary",), vmem_limit_bytes=VMEM_LIMIT
        ),
        cost_estimate=pl.CostEstimate(
            flops=10 * HALF_KV * wide * keys * HEAD_WIDTH,
            bytes_accessed=6 << 20,
            transcendentals=HALF_KV * wide * keys,
        ),
        name="attention_heavy" if heavy else "attention_light",
    )(flags, table, *operands)


def finish_kernel(flags_ref, table_ref, cos_ref, sin_ref, *refs):
    light_keep, heavy_keep, light_from, heavy_from, side_ref, cross_ref, gk_ref, gv_ref = refs
    for place, (keep_ref, from_ref) in enumerate(
        ((light_keep, light_from), (heavy_keep, heavy_from))
    ):
        total = keep_ref[0] + from_ref[0].astype(jnp.float32) + side_ref[place].astype(jnp.float32)
        if place == 0:
            total += cross_ref[...].astype(jnp.float32)
        for sub in range(HALF_KV):
            columns = columns_of(head_of(flags_ref, table_ref[2 + place], sub))
            dk = total[sub * TOK_DEV : (sub + 1) * TOK_DEV] * SCORE_SCALE
            turned = dk * cos_ref[...] + pltpu.roll(dk, HEAD_WIDTH // 2, 1) * sin_ref[...]
            gk_ref[:, columns] = turned.astype(jnp.bfloat16)
            dv = total[(2 + sub) * TOK_DEV : (3 + sub) * TOK_DEV]
            gv_ref[:, columns] = dv.astype(jnp.bfloat16)


def finish(flags, table, cosine, sine, light_keep, heavy_keep, pair_from, side_back, cross_back):
    tok = TOK_DEV

    def whole(shape):
        return pl.BlockSpec(shape, lambda i, f, t: (0,) * len(shape))

    def block(at):
        return pl.BlockSpec((1, 4 * tok, HEAD_WIDTH), lambda i, f, t: (at, 0, 0))

    shape = jax.ShapeDtypeStruct((tok, KEY_VALUE_HEADS * HEAD_WIDTH), jnp.bfloat16)
    return pl.pallas_call(
        finish_kernel,
        grid_spec=pltpu.PrefetchScalarGridSpec(
            num_scalar_prefetch=2,
            grid=(1,),
            in_specs=[whole((tok, HEAD_WIDTH))] * 2
            + [block(0), block(0), block(0), block(2)]
            + [whole(side_back.shape), whole(cross_back.shape)],
            out_specs=[whole(shape.shape)] * 2,
        ),
        out_shape=[shape, shape],
        compiler_params=pltpu.CompilerParams(vmem_limit_bytes=VMEM_LIMIT),
        cost_estimate=pl.CostEstimate(
            flops=20_000_000_000, bytes_accessed=64 << 20, transcendentals=0
        ),
        name="finish_keys_values",
    )(flags, table, cosine, sine, light_keep, heavy_keep, pair_from, pair_from, side_back, cross_back)


def exchange(array, axes):
    return lax.all_to_all(array, axes, 0, 0)


def to_all(array, axes):
    count = lax.axis_size(axes)
    return exchange(jnp.broadcast_to(array[None], (count,) + array.shape), axes)


def add_up(array):
    return jnp.sum(array.astype(jnp.float32), axis=0).astype(jnp.bfloat16)


def local(query, keys, values, out_grad, query_lowrank_state, value_lowrank_state, shift_flags):
    ctx_index = lax.axis_index(SEQ_AXES)
    ctx_count = lax.axis_size(SEQ_AXES)

    def send(array, to):
        pairs = [(i, to(i) % ctx_count) for i in range(ctx_count) if to(i) is not None]
        return lax.ppermute(array, SEQ_AXES, pairs)

    def flip(mask):
        return lambda i: i ^ mask

    def to_odd(i):
        return i + 2 if i // 2 % 2 == 0 else None

    def to_even(i):
        return i - 2 if i // 2 % 2 == 1 else None

    chip = ctx_index // 2
    light_half = chip // 2 % 2
    table = jnp.stack([chip % 2, ctx_index % 2, light_half, 1 - light_half]).astype(jnp.int32)

    both, light = pack(shift_flags, keys[0], values[0], value_lowrank_state[0].T)
    crossed = send(light, lambda i: i + GROUP_DEV // 2)
    sided = send(both, to_odd)
    half_dim = HEAD_WIDTH // 2
    positions = ctx_index * TOK_DEV + jnp.arange(TOK_DEV, dtype=jnp.int32)
    inv_freq = 10000.0 ** (-(jnp.arange(half_dim, dtype=jnp.float32) * 2.0) / HEAD_WIDTH)
    angles = positions.astype(jnp.float32)[:, None] * inv_freq[None, :]
    cos_half, sin_half = jnp.cos(angles), jnp.sin(angles)
    cosine = jnp.concatenate([cos_half, cos_half], axis=1)
    sine = jnp.concatenate([sin_half, -sin_half], axis=1)
    low = query_lowrank_state[0].T
    light_rows, heavy_rows = stage(shift_flags, table, query[0], out_grad[0])
    crossed, sided, cosine, sine, low, light_rows, heavy_rows = lax.optimization_barrier(
        (crossed, sided, cosine, sine, low, light_rows, heavy_rows)
    )
    crossed = crossed[None]
    swapped = send(crossed, flip(2))
    arrived = send(jnp.concatenate([both, sided, crossed]), flip(1))
    swapped_other = send(crossed, flip(3))
    gq, terms, light_keep, light_send = attention(
        False, shift_flags, table, light_rows,
        [(both, 0), (sided, 0)], [(arrived, 0), (arrived, 2)],
        cosine, sine, low, None,
    )
    gq, terms, heavy_keep, pair_send = attention(
        True, shift_flags, table, heavy_rows,
        [(both, 1), (crossed, 0), (swapped, 0), (sided, 1)],
        [(arrived, 1), (arrived, 4), (swapped_other, 0), (arrived, 3)],
        cosine, sine, low, (gq, terms, light_send),
    )

    def wide(array):
        return array.astype(jnp.float32)

    def sent(array):
        return array.astype(jnp.bfloat16)

    terms = exchange(terms, "zc")
    pair_from = send(pair_send, flip(1))
    swap_from = send(sent(heavy_keep[2] + wide(pair_from[4])), flip(2))
    terms, pair_from, swap_from = lax.optimization_barrier((terms, pair_from, swap_from))
    cross_back = send(
        sent(heavy_keep[1] + wide(pair_from[3]) + wide(swap_from)), lambda i: i - GROUP_DEV // 2
    )
    side_back = send(
        sent(jnp.stack([light_keep[1] + wide(pair_from[1]), heavy_keep[3] + wide(pair_from[5])])),
        to_even,
    )
    terms = to_all(add_up(terms)[:TERM_USED], SUM_AXES)
    gk, gv = finish(
        shift_flags, table, cosine, sine, light_keep, heavy_keep, pair_from, side_back, cross_back
    )
    terms = to_all(add_up(terms), "zc")
    query_terms = terms[:, : TERM_HEADS * RANK].reshape(QUERY_HEADS_HALF, RANK, HEAD_WIDTH)
    value_terms = terms[:, TERM_HEADS * RANK :].reshape(KEY_VALUE_HEADS, RANK, HEAD_WIDTH)

    def rank_rows(heads):
        return wide(jnp.transpose(heads, (1, 0, 2)).reshape(RANK, -1))

    return gq[None], gk[None], gv[None], rank_rows(query_terms), rank_rows(value_terms)


def solution(mesh):
    dp, ctx = mesh.shape["dp"], mesh.shape["ctx"]
    split = Mesh(mesh.devices.reshape(dp, ctx // PEERS, PEERS), ("dp", "yh", "zc"))
    rows = P("dp", SEQ_AXES, None)
    return jax.shard_map(
        local,
        mesh=split,
        in_specs=(rows,) * 6 + (P(),),
        out_specs=(rows, rows, rows, P(), P()),
        check_vma=False,
    )
```

```python
from functools import partial
import math

import jax
import jax.numpy as jnp
from jax import lax
from jax.experimental import pallas as pl
from jax.experimental.pallas import tpu as pltpu
from jax.sharding import Mesh, PartitionSpec as P

QUERY_HEADS_HALF = 32
KEY_VALUE_HEADS = 4
HEAD_WIDTH = 128
GROUP_DEV = 8
TOK_DEV = 128
HALF_KV = KEY_VALUE_HEADS // 2
PER_GROUP = QUERY_HEADS_HALF // KEY_VALUE_HEADS
RANK = 8
PACK_ROWS = 4 * TOK_DEV + 16
PEERS = 16
TERM_ROWS = 32
TERM_HEADS = QUERY_HEADS_HALF // PEERS
TERM_USED = TERM_HEADS * (RANK + 1)
ADAPTER_SCALE = 2.0
SCORE_SCALE = 1.0 / math.sqrt(HEAD_WIDTH)
EXP2_SCALE = SCORE_SCALE * math.log2(math.e)
MASKED = -1e30
NT = (((1,), (1,)), ((), ()))
TN = (((0,), (0,)), ((), ()))
VMEM_LIMIT = 20 * 1024 * 1024
SEQ_AXES = ("yh", "zc")
SUM_AXES = ("dp", "yh")


def head_of(flags, half, sub, first=0):
    hit = [flags[first + head] == half for head in range(KEY_VALUE_HEADS)]
    low = jnp.where(hit[0], 0, jnp.where(hit[1], 1, 2))
    high = jnp.where(hit[3], 3, jnp.where(hit[2], 2, 1))
    return jnp.where(sub == 0, low, high)


def columns_of(head):
    return pl.ds(pl.multiple_of(head * HEAD_WIDTH, HEAD_WIDTH), HEAD_WIDTH)


def pack_kernel(flags_ref, keys_ref, values_ref, low_ref, both_ref, light_ref):
    light_half = lax.axis_index("zc") // 4 % 2
    low = low_ref[...].astype(jnp.float32)
    low = jnp.concatenate([low, jnp.zeros_like(low)], axis=0).astype(jnp.bfloat16)
    for place in range(2):
        half = 1 - light_half if place else light_half
        for sub in range(HALF_KV):
            columns = columns_of(head_of(flags_ref, half, sub))
            for kind, ref in enumerate((keys_ref, values_ref)):
                rows = slice((2 * kind + sub) * TOK_DEV, (2 * kind + sub + 1) * TOK_DEV)
                both_ref[place, rows, :] = ref[:, columns]
                if place == 0:
                    light_ref[rows, :] = ref[:, columns]
        both_ref[place, 4 * TOK_DEV :, :] = low
    light_ref[4 * TOK_DEV :, :] = low


def pack(flags, keys, values, low):
    whole = pl.BlockSpec(memory_space=pltpu.VMEM)
    scalars = pl.BlockSpec(memory_space=pltpu.SMEM)
    return pl.pallas_call(
        pack_kernel,
        out_shape=(
            jax.ShapeDtypeStruct((2, PACK_ROWS, HEAD_WIDTH), jnp.bfloat16),
            jax.ShapeDtypeStruct((PACK_ROWS, HEAD_WIDTH), jnp.bfloat16),
        ),
        in_specs=[scalars, whole, whole, whole],
        out_specs=(whole, whole),
        name="pack_heads",
    )(flags, keys, values, low)


def stage_kernel(table_ref, query_ref, out_grad_ref, *outs):
    for place in range(2):
        for sub in range(HALF_KV):
            head = head_of(table_ref, table_ref[2 + place], sub, 4)
            for h in range(PER_GROUP):
                start = (sub * PER_GROUP + h) * TOK_DEV
                for kind, ref in enumerate((query_ref, out_grad_ref)):
                    outs[2 * place + kind][start : start + TOK_DEV, :] = ref[
                        :, columns_of(head * PER_GROUP + h)
                    ]


def stage(table, query, out_grad):
    whole = pl.BlockSpec(memory_space=pltpu.VMEM)
    scalars = pl.BlockSpec(memory_space=pltpu.SMEM)
    shape = jax.ShapeDtypeStruct((HALF_KV * PER_GROUP * TOK_DEV, HEAD_WIDTH), jnp.bfloat16)
    outs = pl.pallas_call(
        stage_kernel,
        out_shape=[shape] * 4,
        in_specs=[scalars, whole, whole],
        out_specs=[whole] * 4,
        compiler_params=pltpu.CompilerParams(vmem_limit_bytes=VMEM_LIMIT),
        name="stage_rows",
    )(table, query, out_grad)
    return outs[:2], outs[2:]


def attention_kernel(heavy, table_ref, q_ref, d_ref, *refs):
    chunks = 4 if heavy else 2
    mine, other = refs[:chunks], refs[chunks : 2 * chunks]
    cos_ref, sin_ref, low_ref = refs[2 * chunks : 2 * chunks + 3]
    before_ref = refs[2 * chunks + 3] if heavy else None
    gq_ref, term_ref, keep_ref, send_ref = refs[len(refs) - 9 : len(refs) - 5]
    k_all, v_all, low_all, dk_ref, dv_ref = refs[len(refs) - 5 :]
    sub = pl.program_id(0)
    odd, core = table_ref[0], table_ref[1]
    rows = 2 * TOK_DEV
    tiles = 1 if heavy else 2
    part = PER_GROUP * TOK_DEV // tiles
    k_rows = pl.ds(pl.multiple_of(sub * TOK_DEV, TOK_DEV), TOK_DEV)
    v_rows = pl.ds(pl.multiple_of((2 + sub) * TOK_DEV, TOK_DEV), TOK_DEV)

    def branch(n):
        for j in range(n):
            for c, side in enumerate((mine[j], other[j])):
                span = slice(j * rows + c * TOK_DEV, j * rows + (c + 1) * TOK_DEV)
                k_all[span, :] = side[0, k_rows, :]
                v_all[span, :] = side[0, v_rows, :]
                low_all[:, span] = side[0, 4 * TOK_DEV :, :]
        width = n * rows
        key = lax.broadcasted_iota(jnp.int32, (rows, part), 0)
        row = lax.broadcasted_iota(jnp.int32, (rows, part), 1) % TOK_DEV
        limit = jnp.where(core == 1, rows, 0)
        allowed = (key <= row) | ((key >= TOK_DEV) & (key < limit))

        k = k_all[:width, :]
        v = v_all[:width, :]

        def products(t):
            q, d = (ref[t * part : (t + 1) * part, :] for ref in (q_ref, d_ref))
            s = lax.dot_general(k, q, NT, preferred_element_type=jnp.float32)
            near = jnp.where(allowed, s[:rows], MASKED)
            s = near if n == 1 else jnp.concatenate([near, s[rows:]], axis=0)
            dp = lax.dot_general(v, d, NT, preferred_element_type=jnp.float32)
            top = jnp.max(s, axis=0, keepdims=True) * EXP2_SCALE
            p = jnp.exp2(s * EXP2_SCALE - top)
            inverse = 1.0 / jnp.sum(p, axis=0, keepdims=True)
            delta = jnp.sum(p * dp, axis=0, keepdims=True) * inverse
            p = p * inverse
            ds = (p * (dp - delta)).astype(jnp.bfloat16)
            return q, d, p.astype(jnp.bfloat16), ds

        dqs = []
        ahead = products(0)
        for t in range(tiles):
            q, d, p, ds = ahead
            if t + 1 < tiles:
                ahead = products(t + 1)
            dv = jnp.dot(p, d, preferred_element_type=jnp.float32)
            dk = jnp.dot(ds, q, preferred_element_type=jnp.float32)
            if t == 0:
                dv_ref[:width, :] = dv
                dk_ref[:width, :] = dk
            else:
                dv_ref[:width, :] += dv
                dk_ref[:width, :] += dk
            dqs.append(lax.dot_general(ds, k, TN, preferred_element_type=jnp.float32))
        dq = jnp.concatenate(dqs, axis=0) * SCORE_SCALE
        low_rank = low_ref[...]
        parts = []
        for h in range(PER_GROUP):
            x = dq[h * TOK_DEV : (h + 1) * TOK_DEV, :]
            turned = x * cos_ref[...] + pltpu.roll(x, HEAD_WIDTH // 2, 1) * sin_ref[...]
            low = turned.astype(jnp.bfloat16)
            gq_ref[:, h * HEAD_WIDTH : (h + 1) * HEAD_WIDTH] = low
            parts.append(
                jnp.dot(low_rank, low, preferred_element_type=jnp.float32) * ADAPTER_SCALE
            )
        value_part = (
            jnp.dot(
                low_all[:, :width],
                dv_ref[:width, :].astype(jnp.bfloat16),
                preferred_element_type=jnp.float32,
            )
            * ADAPTER_SCALE
        )
        blank = jnp.zeros((TERM_ROWS - TERM_USED, HEAD_WIDTH), jnp.float32)
        for i in range(PER_GROUP // TERM_HEADS):
            these = slice(i * TERM_HEADS, (i + 1) * TERM_HEADS)
            block = jnp.concatenate([*parts[these], value_part[these], blank], axis=0)
            term_ref[i] = block.astype(jnp.bfloat16)

        def store(ref, j, span):
            for grad_ref, to_rows in ((dk_ref, k_rows), (dv_ref, v_rows)):
                if j < n:
                    grad = grad_ref[j * rows + span * TOK_DEV : j * rows + (span + 1) * TOK_DEV, :]
                else:
                    grad = jnp.zeros((TOK_DEV, HEAD_WIDTH), jnp.float32)
                ref[to_rows, :] = grad.astype(ref.dtype)

        first = 2 if heavy else 0
        for j in range(chunks):
            store(keep_ref.at[j], j, 0)
            store(send_ref.at[first + j], j, 1)

    if heavy:

        @pl.when(sub == 0)
        def _():
            send_ref[:2] = before_ref[...]

    base = 3 if heavy else 1
    for more in range(2):
        pl.when(odd == more)(lambda n=base + more: branch(n))


def attention(heavy, table, rows, mine, other, cosine, sine, low, before):
    tok = TOK_DEV
    wide = PER_GROUP * HEAD_WIDTH
    chunks = len(mine)
    keys = chunks * 2 * tok
    place = 1 if heavy else 0

    def whole(shape):
        return pl.BlockSpec(shape, lambda s, t: (0,) * len(shape))

    def head(t, s):
        return head_of(t, t[2 + place], s, 4)

    columns = pl.BlockSpec((tok, wide), lambda s, t: (0, head(t, s)))
    terms = pl.BlockSpec((PER_GROUP // TERM_HEADS, TERM_ROWS, HEAD_WIDTH), lambda s, t: (head(t, s), 0, 0))
    table_spec = whole((tok, HEAD_WIDTH))
    stacked = pl.BlockSpec((wide, HEAD_WIDTH), lambda s, t: (s, 0))
    in_specs = [stacked, stacked]
    for array, at in (*mine, *other):
        in_specs.append(
            pl.BlockSpec((1, PACK_ROWS, HEAD_WIDTH), lambda s, t, at=at: (at, 0, 0))
        )
    in_specs += [table_spec, table_spec, whole((RANK, tok))]
    operands = [*rows, *(array for array, at in (*mine, *other)), cosine, sine, low]
    aliases = {}
    if heavy:
        *before, light_send = before
        operands.append(light_send)
        in_specs.append(whole(light_send.shape))
        for out, array in enumerate(before):
            aliases[1 + len(operands)] = out
            operands.append(array)
            in_specs.append(pl.BlockSpec(memory_space=pl.ANY))
    out_shape = [
        jax.ShapeDtypeStruct((tok, QUERY_HEADS_HALF * HEAD_WIDTH), jnp.bfloat16),
        jax.ShapeDtypeStruct((PEERS, TERM_ROWS, HEAD_WIDTH), jnp.bfloat16),
        jax.ShapeDtypeStruct((chunks, 4 * tok, HEAD_WIDTH), jnp.float32),
        jax.ShapeDtypeStruct((6 if heavy else 2, 4 * tok, HEAD_WIDTH), jnp.bfloat16),
    ]
    return pl.pallas_call(
        partial(attention_kernel, heavy),
        grid_spec=pltpu.PrefetchScalarGridSpec(
            num_scalar_prefetch=1,
            grid=(HALF_KV,),
            in_specs=in_specs,
            out_specs=[columns, terms] + [whole(o.shape) for o in out_shape[2:]],
            scratch_shapes=[
                pltpu.VMEM((keys, HEAD_WIDTH), jnp.bfloat16),
                pltpu.VMEM((keys, HEAD_WIDTH), jnp.bfloat16),
                pltpu.VMEM((16, keys), jnp.bfloat16),
                pltpu.VMEM((keys, HEAD_WIDTH), jnp.float32),
                pltpu.VMEM((keys, HEAD_WIDTH), jnp.float32),
            ],
        ),
        out_shape=out_shape,
        input_output_aliases=aliases,
        compiler_params=pltpu.CompilerParams(
            dimension_semantics=("arbitrary",), vmem_limit_bytes=VMEM_LIMIT
        ),
        cost_estimate=pl.CostEstimate(
            flops=10 * HALF_KV * wide * keys * HEAD_WIDTH,
            bytes_accessed=6 << 20,
            transcendentals=HALF_KV * wide * keys,
        ),
        name="attention_heavy" if heavy else "attention_light",
    )(table, *operands)


def finish_kernel(table_ref, cos_ref, sin_ref, *refs):
    light_keep, heavy_keep, light_from, heavy_from, side_ref, cross_ref, gk_ref, gv_ref = refs
    for place, (keep_ref, from_ref) in enumerate(
        ((light_keep, light_from), (heavy_keep, heavy_from))
    ):
        total = keep_ref[0] + from_ref[0].astype(jnp.float32) + side_ref[place].astype(jnp.float32)
        if place == 0:
            total += cross_ref[...].astype(jnp.float32)
        for sub in range(HALF_KV):
            columns = columns_of(head_of(table_ref, table_ref[2 + place], sub, 4))
            dk = total[sub * TOK_DEV : (sub + 1) * TOK_DEV] * SCORE_SCALE
            turned = dk * cos_ref[...] + pltpu.roll(dk, HEAD_WIDTH // 2, 1) * sin_ref[...]
            gk_ref[:, columns] = turned.astype(jnp.bfloat16)
            dv = total[(2 + sub) * TOK_DEV : (3 + sub) * TOK_DEV]
            gv_ref[:, columns] = dv.astype(jnp.bfloat16)


def finish(table, cosine, sine, light_keep, heavy_keep, pair_from, side_back, cross_back):
    tok = TOK_DEV

    def whole(shape):
        return pl.BlockSpec(shape, lambda i, t: (0,) * len(shape))

    def block(at):
        return pl.BlockSpec((1, 4 * tok, HEAD_WIDTH), lambda i, t: (at, 0, 0))

    shape = jax.ShapeDtypeStruct((tok, KEY_VALUE_HEADS * HEAD_WIDTH), jnp.bfloat16)
    return pl.pallas_call(
        finish_kernel,
        grid_spec=pltpu.PrefetchScalarGridSpec(
            num_scalar_prefetch=1,
            grid=(1,),
            in_specs=[whole((tok, HEAD_WIDTH))] * 2
            + [block(0), block(0), block(0), block(2)]
            + [whole(side_back.shape), whole(cross_back.shape)],
            out_specs=[whole(shape.shape)] * 2,
        ),
        out_shape=[shape, shape],
        compiler_params=pltpu.CompilerParams(vmem_limit_bytes=VMEM_LIMIT),
        cost_estimate=pl.CostEstimate(
            flops=20_000_000_000, bytes_accessed=64 << 20, transcendentals=0
        ),
        name="finish_keys_values",
    )(table, cosine, sine, light_keep, heavy_keep, pair_from, pair_from, side_back, cross_back)


def exchange(array, axes):
    return lax.all_to_all(array, axes, 0, 0)


def to_all(array, axes):
    count = lax.axis_size(axes)
    return exchange(jnp.broadcast_to(array[None], (count,) + array.shape), axes)


def add_up(array):
    return jnp.sum(array.astype(jnp.float32), axis=0).astype(jnp.bfloat16)


def local(query, keys, values, out_grad, query_lowrank_state, value_lowrank_state, shift_flags):
    ctx_index = lax.axis_index(SEQ_AXES)
    ctx_count = lax.axis_size(SEQ_AXES)

    def send(array, to):
        pairs = [(i, to(i) % ctx_count) for i in range(ctx_count) if to(i) is not None]
        return lax.ppermute(array, SEQ_AXES, pairs)

    def flip(mask):
        return lambda i: i ^ mask

    def to_odd(i):
        return i + 2 if i // 2 % 2 == 0 else None

    def to_even(i):
        return i - 2 if i // 2 % 2 == 1 else None

    chip = ctx_index // 2
    light_half = chip // 2 % 2
    table = jnp.stack([chip % 2, ctx_index % 2, light_half, 1 - light_half]).astype(jnp.int32)
    table = jnp.concatenate([table, shift_flags])

    both, light = pack(shift_flags, keys[0], values[0], value_lowrank_state[0].T)
    crossed = send(light, lambda i: i + GROUP_DEV // 2)
    sided = send(both, to_odd)
    half_dim = HEAD_WIDTH // 2
    positions = ctx_index * TOK_DEV + jnp.arange(TOK_DEV, dtype=jnp.int32)
    inv_freq = 10000.0 ** (-(jnp.arange(half_dim, dtype=jnp.float32) * 2.0) / HEAD_WIDTH)
    angles = positions.astype(jnp.float32)[:, None] * inv_freq[None, :]
    cos_half, sin_half = jnp.cos(angles), jnp.sin(angles)
    cosine = jnp.concatenate([cos_half, cos_half], axis=1)
    sine = jnp.concatenate([sin_half, -sin_half], axis=1)
    low = query_lowrank_state[0].T
    light_rows, heavy_rows = stage(table, query[0], out_grad[0])
    crossed, sided, cosine, sine, low, light_rows, heavy_rows = lax.optimization_barrier(
        (crossed, sided, cosine, sine, low, light_rows, heavy_rows)
    )
    crossed = crossed[None]
    swapped = send(crossed, flip(2))
    arrived = send(jnp.concatenate([both, sided, crossed]), flip(1))
    swapped_other = send(crossed, flip(3))
    gq, terms, light_keep, light_send = attention(
        False, table, light_rows,
        [(both, 0), (sided, 0)], [(arrived, 0), (arrived, 2)],
        cosine, sine, low, None,
    )
    gq, terms, heavy_keep, pair_send = attention(
        True, table, heavy_rows,
        [(both, 1), (crossed, 0), (swapped, 0), (sided, 1)],
        [(arrived, 1), (arrived, 4), (swapped_other, 0), (arrived, 3)],
        cosine, sine, low, (gq, terms, light_send),
    )

    def wide(array):
        return array.astype(jnp.float32)

    def sent(array):
        return array.astype(jnp.bfloat16)

    terms = exchange(terms, "zc")
    pair_from = send(pair_send, flip(1))
    swap_from = send(sent(heavy_keep[2] + wide(pair_from[4])), flip(2))
    terms, pair_from, swap_from = lax.optimization_barrier((terms, pair_from, swap_from))
    cross_back = send(
        sent(heavy_keep[1] + wide(pair_from[3]) + wide(swap_from)), lambda i: i - GROUP_DEV // 2
    )
    side_back = send(
        sent(jnp.stack([light_keep[1] + wide(pair_from[1]), heavy_keep[3] + wide(pair_from[5])])),
        to_even,
    )
    terms = to_all(add_up(terms)[:TERM_USED], SUM_AXES)
    gk, gv = finish(
        table, cosine, sine, light_keep, heavy_keep, pair_from, side_back, cross_back
    )
    terms = to_all(add_up(terms), "zc")
    query_terms = terms[:, : TERM_HEADS * RANK].reshape(QUERY_HEADS_HALF, RANK, HEAD_WIDTH)
    value_terms = terms[:, TERM_HEADS * RANK :].reshape(KEY_VALUE_HEADS, RANK, HEAD_WIDTH)

    def rank_rows(heads):
        return wide(jnp.transpose(heads, (1, 0, 2)).reshape(RANK, -1))

    return gq[None], gk[None], gv[None], rank_rows(query_terms), rank_rows(value_terms)


def solution(mesh):
    dp, ctx = mesh.shape["dp"], mesh.shape["ctx"]
    split = Mesh(mesh.devices.reshape(dp, ctx // PEERS, PEERS), ("dp", "yh", "zc"))
    rows = P("dp", SEQ_AXES, None)
    return jax.shard_map(
        local,
        mesh=split,
        in_specs=(rows,) * 6 + (P(),),
        out_specs=(rows, rows, rows, P(), P()),
        check_vma=False,
    )
```
